256 devices in a mesh: gx: 32 (over y_lo, z, core), gy: 8 (over y_hi, x).
Axes of the slice: x: 4, y: 4 (y_hi: 2, y_lo: 2; y = y_hi * 2 + y_lo), z: 8, core: 2. Of those that a mesh axis runs over, the one named last changes fastest.
Arguments:
- populations: bfloat16 [19, 16, 512, 2048], P(None, None, 'gx', 'gy'), may hold values from 0 to 1, as said below
Outputs:
- advanced: float32 [19, 16, 512, 2048], P(None, None, 'gx', 'gy')
The draws below stay inside these ranges and needn't reach their ends.
Inputs may be any that keep to these rules, and one draw needn't show every extreme that they name: `populations`: every population is positive.
All inputs are finite; a program needn't handle non-finite values.
Results may differ from the reference program's by a relative error of at most 0.0003.
Values sent between devices are 32-bit elements; how exact they have to be, the bound alone decides.
No kernel may reach another device: no remote copies, remote signals or barrier semaphores. Data moves between devices by JAX's collectives and lax.ppermute only.
A program may use at most 64 MiB of HBM per device.

```python
import math
import jax
import jax.numpy as jnp

NZ = 16
STEPS = 2
NX = 512
NY = 2048


def draw_populations(key, part):
    key = jax.random.fold_in(key, 7)
    first, second, third = jax.random.split(key, 3)
    weights = jnp.array([1.0 / 3.0] + [1.0 / 18.0] * 6 + [1.0 / 36.0] * 12, jnp.float32)
    phase = jax.random.uniform(third, (NZ, NX, NY), jnp.float32, 0.0, 1.0) < 0.5
    level = jax.random.uniform(first, (NZ, NX, NY), jnp.float32, 0.0, 1.0)
    dense = jnp.exp(level * math.log(1.5))
    light = jnp.exp(math.log(0.3) + level * (math.log(0.5) - math.log(0.3)))
    density = jnp.where(phase, dense, light)
    noise = 0.6 * jnp.clip(jax.random.normal(second, (19, NZ, NX, NY), jnp.float32) * 0.5, -1.0, 1.0)
    values = weights[:, None, None, None] * density[None] * (1.0 + noise)
    return values.astype(jnp.bfloat16)


def setup_inputs(seed: int = 0) -> dict:
    key_of = jax.random.split(jax.random.key(seed), 2)
    return {
        "populations": draw_populations(jax.random.fold_in(key_of[1], 71), 0),
    }


VELOCITY = ((0, 0, 0), (1, 0, 0), (-1, 0, 0), (0, 1, 0), (0, -1, 0), (0, 0, 1), (0, 0, -1),
            (1, 1, 0), (-1, -1, 0), (1, -1, 0), (-1, 1, 0), (1, 0, 1), (-1, 0, -1), (1, 0, -1),
            (-1, 0, 1), (0, 1, 1), (0, -1, -1), (0, 1, -1), (0, -1, 1))
WEIGHT = (1.0 / 3.0,) + (1.0 / 18.0,) * 6 + (1.0 / 36.0,) * 12
coupling = -6.0


def lattice_step(current):
    floats = current.astype(jnp.float32)
    rho = jnp.sum(floats, axis=0)
    psi = 1.0 - jnp.exp(-rho)
    zeros = jnp.zeros_like(rho)
    acc_x, acc_y, acc_z = zeros, zeros, zeros
    mom_x, mom_y, mom_z = zeros, zeros, zeros
    for index in range(1, 19):
        ex, ey, ez = VELOCITY[index]
        weight = WEIGHT[index]
        neighbour = jnp.roll(psi, (-ez, -ex, -ey), (0, 1, 2))
        acc_x = acc_x + weight * ex * neighbour
        acc_y = acc_y + weight * ey * neighbour
        acc_z = acc_z + weight * ez * neighbour
        mom_x = mom_x + ex * floats[index]
        mom_y = mom_y + ey * floats[index]
        mom_z = mom_z + ez * floats[index]
    scale = -coupling * psi
    vel_x = (mom_x + scale * acc_x) / rho
    vel_y = (mom_y + scale * acc_y) / rho
    vel_z = (mom_z + scale * acc_z) / rho
    square = vel_x * vel_x + vel_y * vel_y + vel_z * vel_z
    read = []
    for index in range(19):
        ex, ey, ez = VELOCITY[index]
        along = ex * vel_x + ey * vel_y + ez * vel_z
        equil = WEIGHT[index] * rho * (1.0 + 3.0 * along + 4.5 * along * along - 1.5 * square)
        read.append(jnp.roll(equil, (ez, ex, ey), (0, 1, 2)))
    return jnp.stack(read, axis=0)


def reference(populations):
    current = populations.astype(jnp.float32)
    for step in range(STEPS):
        current = lattice_step(current)
    return current
```

```python
import jax
import jax.numpy as jnp
from jax import lax
from jax.experimental import pallas as pl
from jax.experimental.pallas import tpu as pltpu
from jax.sharding import PartitionSpec as P

HALO = 4
LANES = 128


def pair_swap(array, axis, odd):
    size = lax.axis_size(axis)
    pairs = []
    for low in range(odd, size + odd, 2):
        a, b = low % size, (low + 1) % size
        pairs += [(a, b), (b, a)]
    return lax.ppermute(array, axis, pairs)


def iota(shape, dim):
    return lax.broadcasted_iota(jnp.int32, shape, dim)


def moments_kernel(nz, chunks, par_ref, pop_ref, m_ref, o_ref, sa_ref, sb_ref, buf, sems):
    step = nz // chunks
    half = nz // 2
    copies = []
    for c in range(chunks):
        part = pl.ds(c * step, step)
        copies.append(pltpu.make_async_copy(pop_ref.at[:, part], buf.at[:, part], sems.at[c]))
        copies[-1].start()
    even = par_ref[0] == 0
    rows = buf.shape[2]
    lane = iota((rows, LANES), 1)
    sub = iota((8, LANES), 0)
    keep = (sub >= HALO) == even

    def plane(z, packed, upper):
        tiles = []
        for lt in range(2):
            cols = slice(lt * LANES, (lt + 1) * LANES)

            def f(i):
                return buf[i, z, :, cols].astype(jnp.float32)

            rho, jx, jy, jz = f(0), None, None, None
            f1, f2 = f(1), f(2)
            rho, jx = rho + (f1 + f2), f1 - f2
            f1, f2 = f(3), f(4)
            rho, jy = rho + (f1 + f2), f1 - f2
            f1, f2 = f(5), f(6)
            rho, jz = rho + (f1 + f2), f1 - f2
            f1, f2 = f(7), f(8)
            d = f1 - f2
            rho, jx, jy = rho + (f1 + f2), jx + d, jy + d
            f1, f2 = f(9), f(10)
            d = f1 - f2
            rho, jx, jy = rho + (f1 + f2), jx + d, jy - d
            f1, f2 = f(11), f(12)
            d = f1 - f2
            rho, jx, jz = rho + (f1 + f2), jx + d, jz + d
            f1, f2 = f(13), f(14)
            d = f1 - f2
            rho, jx, jz = rho + (f1 + f2), jx + d, jz - d
            f1, f2 = f(15), f(16)
            d = f1 - f2
            rho, jy, jz = rho + (f1 + f2), jy + d, jz + d
            f1, f2 = f(17), f(18)
            d = f1 - f2
            rho, jy, jz = rho + (f1 + f2), jy + d, jz - d
            tiles.append((rho, jx, jy, jz))
        out = []
        shift = lax.rem(z * 8 + 4, LANES)
        for k in range(4):
            both = jnp.where(lane >= LANES - HALO, tiles[1][k], tiles[0][k])
            out.append(jnp.where(lane // 8 == z, pltpu.roll(both, shift, 1), packed[k]))
            for lt in range(2):
                v = tiles[lt][k]
                m_ref[k, z, :, lt * LANES : (lt + 1) * LANES] = v
                low, high = v[:8], v[rows - 8 :]
                va = jnp.where(even, high, low)
                vb = jnp.where(even, low, high)
                if upper:
                    slot = lt * half + z - half
                    va, vb = pltpu.roll(va, HALO, 0), pltpu.roll(vb, HALO, 0)
                    va = jnp.where(keep, sa_ref[k, slot], va)
                    vb = jnp.where(keep, vb, sb_ref[k, slot])
                else:
                    slot = lt * half + z
                sa_ref[k, slot] = va
                sb_ref[k, slot] = vb
        return tuple(out)

    packed = (jnp.zeros((rows, LANES), jnp.float32),) * 4
    for c in range(chunks):
        copies[c].wait()
        upper = c * step >= half
        packed = lax.fori_loop(
            c * step, (c + 1) * step, lambda z, t, upper=upper: plane(z, t, upper), packed
        )
    for k in range(4):
        o_ref[k] = packed[k]


def strips_of(o, oa, ob, even):
    own = (iota(o.shape, 1) & 7) < HALO
    right = jnp.where(even, oa, ob)
    left = jnp.where(even, ob, oa)
    return jnp.where(own, left, o), jnp.where(own, o, right)


def corner_kernel(par_ref, o_ref, oa_ref, ob_ref, sa_in, sb_in, sa_ref, sb_ref, tiles, sems):
    del sa_in, sb_in
    even = par_ref[0] == 0
    rows = o_ref.shape[1]
    slot = sa_ref.shape[1] - 1
    keep = (iota((8, LANES), 0) >= HALO) == even
    for k in range(4):
        ls, rs = strips_of(o_ref[k], oa_ref[k], ob_ref[k], par_ref[1] == 0)
        la, lb = jnp.where(even, ls[rows - 8 :], ls[:8]), jnp.where(even, ls[:8], ls[rows - 8 :])
        ra, rb = jnp.where(even, rs[rows - 8 :], rs[:8]), jnp.where(even, rs[:8], rs[rows - 8 :])
        tiles[0, k] = jnp.where(keep, la, pltpu.roll(ra, HALO, 0))
        tiles[1, k] = jnp.where(keep, pltpu.roll(rb, HALO, 0), lb)
    copies = [
        pltpu.make_async_copy(tiles.at[n], ref.at[:, slot], sems.at[n])
        for n, ref in enumerate((sa_ref, sb_ref))
    ]
    for copy in copies:
        copy.start()
    for copy in copies:
        copy.wait()


def xp(v):
    return pltpu.roll(v, v.shape[0] - 1, 0)


def xm(v):
    return pltpu.roll(v, 1, 0)


def density(v):
    return 1.0 - jnp.exp(-v)


def post_of(p, fx, fy, fz, rho, jx, jy, jz):
    inv = 1.0 / rho
    scale = p * (1.0 / 6.0)
    ux = (jx + scale * fx) * inv
    uy = (jy + scale * fy) * inv
    uz = (jz + scale * fz) * inv
    r36 = rho * (1.0 / 36.0)
    r3 = rho * (1.0 / 12.0)
    ox, oy, oz = r3 * ux, r3 * uy, r3 * uz
    hx, hy, hz = 1.5 * ux, 1.5 * uy, 1.5 * uz
    xx, yy, zz = hx * ox, hy * oy, hz * oz
    k = r36 - (xx + yy + zz) * (1.0 / 3.0)
    kx, ky, kz = k + xx, k + yy, k + zz
    out = [12.0 * k]
    for e, o in ((kx, ox), (ky, oy), (kz, oz)):
        e2, o2 = e + e, o + o
        out += [e2 + o2, e2 - o2]
    for e, a, b, h in ((kx + yy, ox, oy, hx), (kx + zz, ox, oz, hx), (ky + zz, oy, oz, hy)):
        cross = h * b
        cross = cross + cross
        ep, em = e + cross, e - cross
        op, om = a + b, a - b
        out += [ep + op, ep - op, em + om, em - om]
    return out


def step_kernel(nz, par_ref, m_ref, o_ref, oa_ref, ob_ref, ha_ref, hb_ref, out_ref,
                e_ref, p_ref, q_ref, d_ref, b_ref, g_ref, st_ref, s1_ref, s2_ref, buf, sems):
    half = nz // 2
    rows = m_ref.shape[2]
    ring = rows + 2 * HALO
    evenx = par_ref[0] == 0
    eveny = par_ref[1] == 0
    sub = iota((8, LANES), 0)
    lane = iota((ring, LANES), 1)
    first, last = lane == 0, lane == LANES - 1

    def halo_tile(k, slot, upper):
        a, b = ha_ref[k, slot], hb_ref[k, slot]
        right, left = jnp.where(evenx, a, b), jnp.where(evenx, b, a)
        if upper:
            return pltpu.roll(jnp.where(sub < HALO, left, right), HALO, 0)
        return jnp.where(sub < HALO, right, left)

    def strip(side):
        v = []
        for k in range(4):
            pair = strips_of(o_ref[k], oa_ref[k], ob_ref[k], eveny)
            tile = halo_tile(k, 2 * half, side == 1)
            v.append(jnp.concatenate([pair[side], tile], axis=0))
        rho, jx, jy, jz = v

        def ym(a):
            return pltpu.roll(a, 1, 1)

        def yp(a):
            return pltpu.roll(a, LANES - 1, 1)

        def zm(a):
            return pltpu.roll(a, 8, 1)

        def zp(a):
            return pltpu.roll(a, LANES - 8, 1)

        def post(p):
            a, b = ym(p), yp(p)
            q, d = p + p + (a + b), b - a
            bb = q + (xp(p) + xm(p))
            aa = q + (zp(p) + zm(p))
            fx = xp(aa) - xm(aa)
            fy = d + d + (xp(d) + xm(d)) + (zp(d) + zm(d))
            fz = zp(bb) - zm(bb)
            return post_of(p, fx, fy, fz, rho, jx, jy, jz)

        p = density(rho)
        st_ref[side] = p
        f = post(p)
        a7, a10, a8, a9 = xm(f[7]), xp(f[10]), xp(f[8]), xm(f[9])
        sp, jp = f[3] + (a7 + a10), a7 - a10
        sn, jn = f[4] + (a8 + a9), a9 - a8
        for n, w in enumerate((sp, jp, f[15], f[17]) if side == 0 else (sn, jn, f[18], f[16])):
            s1_ref[side, n] = w
        a, b = xm(f[1]), xp(f[2])
        sp, jp, sn, jn = ym(sp), ym(jp), yp(sn), yp(jn)
        r0, jx0, jy0 = f[0] + (a + b) + (sp + sn), (a - b) + (jp + jn), sp - sn
        a, b, c, e = xm(f[11]), xp(f[14]), ym(f[15]), yp(f[18])
        ru, jxu, jyu = zm(f[5] + (a + b) + (c + e)), zm(a - b), zm(c - e)
        a, b, c, e = xm(f[13]), xp(f[12]), ym(f[17]), yp(f[16])
        rd, jxd, jyd = zp(f[6] + (a + b) + (c + e)), zp(a - b), zp(c - e)
        rho, jx, jy, jz = r0 + (ru + rd), jx0 + (jxu + jxd), jy0 + (jyu + jyd), ru - rd
        p = density(rho)
        st_ref[2 + side] = p
        f = post(p)
        if side == 0:
            keep = (f[3], xm(f[7]), xp(f[10]), f[15], f[17])
        else:
            keep = (f[4], xp(f[8]), xm(f[9]), f[16], f[18])
        for n, w in enumerate(keep):
            s2_ref[side, n] = w

    strip(0)
    strip(1)

    def cols(lt):
        return slice(lt * LANES, (lt + 1) * LANES)

    def pull_left(z, a0, a1, edge):
        r0, r1 = pltpu.roll(a0, 1, 1), pltpu.roll(a1, 1, 1)
        h = pltpu.roll(edge, LANES - 3 - z * 8, 1)
        f = first[: a0.shape[0]]
        return jnp.where(f, h, r0), jnp.where(f, r0, r1)

    def pull_right(z, a0, a1, edge):
        r0, r1 = pltpu.roll(a0, LANES - 1, 1), pltpu.roll(a1, LANES - 1, 1)
        h = pltpu.roll(edge, LANES - 5 - z * 8, 1)
        f = last[: a0.shape[0]]
        return jnp.where(f, r1, r0), jnp.where(f, h, r1)

    def up(z):
        return (z + 1) & (nz - 1)

    def down(z):
        return (z + nz - 1) & (nz - 1)

    def load(z, upper):
        for lt in range(2):
            slot = lt * half + z - (half if upper else 0)
            for k in range(4):
                tile = halo_tile(k, slot, upper)
                e_ref[k, z, :rows, cols(lt)] = m_ref[k, z, :, cols(lt)]
                e_ref[k, z, rows:, cols(lt)] = tile
                if k == 0:
                    p_ref[z, :rows, cols(lt)] = density(m_ref[0, z, :, cols(lt)])
                    p_ref[z, rows:, cols(lt)] = density(tile)

    def loop(lo, hi, fn):
        lax.fori_loop(lo, hi, lambda z, c: (fn(z), c)[1], 0)

    loop(0, half, lambda z: load(z, False))
    loop(half, nz, lambda z: load(z, True))

    def gradients(step):
        def fn(z):
            p0, p1 = p_ref[z, :, cols(0)], p_ref[z, :, cols(1)]
            a = pull_left(z, p0, p1, st_ref[2 * step])
            b = pull_right(z, p0, p1, st_ref[2 * step + 1])
            for lt, p in enumerate((p0, p1)):
                q = p + p + (a[lt] + b[lt])
                q_ref[z, :, cols(lt)] = q
                d_ref[z, :, cols(lt)] = b[lt] - a[lt]
                b_ref[z, :, cols(lt)] = q + (xp(p) + xm(p))

        loop(0, nz, fn)

    def posts(z, lt):
        c = cols(lt)
        zu, zd = up(z), down(z)
        aa = q_ref[z, :, c] + (p_ref[zu, :, c] + p_ref[zd, :, c])
        fx = xp(aa) - xm(aa)
        d = d_ref[z, :, c]
        fy = d + d + (xp(d) + xm(d)) + (d_ref[zu, :, c] + d_ref[zd, :, c])
        fz = b_ref[zu, :, c] - b_ref[zd, :, c]
        v = [e_ref[k, z, :, c] for k in range(4)]
        return post_of(p_ref[z, :, c], fx, fy, fz, *v)

    def first_step(z):
        parts = []
        for lt in range(2):
            c = cols(lt)
            f = posts(z, lt)
            a7, a10, a8, a9 = xm(f[7]), xp(f[10]), xp(f[8]), xm(f[9])
            left = (f[3] + (a7 + a10), a7 - a10, f[15], f[17])
            right = (f[4] + (a8 + a9), a9 - a8, f[18], f[16])
            a, b = xm(f[1]), xp(f[2])
            g_ref[0, z, :, c] = f[0] + (a + b)
            g_ref[1, z, :, c] = a - b
            a, b = xm(f[11]), xp(f[14])
            g_ref[3, z, :, c] = f[5] + (a + b)
            g_ref[4, z, :, c] = a - b
            a, b = xm(f[13]), xp(f[12])
            g_ref[6, z, :, c] = f[6] + (a + b)
            g_ref[7, z, :, c] = a - b
            parts.append((left, right))
        moved = [
            (
                pull_left(z, parts[0][0][n], parts[1][0][n], s1_ref[0, n]),
                pull_right(z, parts[0][1][n], parts[1][1][n], s1_ref[1, n]),
            )
            for n in range(4)
        ]
        for lt in range(2):
            c = cols(lt)
            sp, sn = moved[0][0][lt], moved[0][1][lt]
            jp, jn = moved[1][0][lt], moved[1][1][lt]
            g_ref[0, z, :, c] += sp + sn
            g_ref[1, z, :, c] += jp + jn
            g_ref[2, z, :, c] = sp - sn
            for n, base in ((2, 3), (3, 6)):
                a, b = moved[n][0][lt], moved[n][1][lt]
                g_ref[base, z, :, c] += a + b
                g_ref[base + 2, z, :, c] = a - b

    def gather(z):
        zu, zd = up(z), down(z)
        for lt in range(2):
            c = cols(lt)
            ru, rd = g_ref[3, zd, :, c], g_ref[6, zu, :, c]
            rho = g_ref[0, z, :, c] + (ru + rd)
            e_ref[0, z, :, c] = rho
            e_ref[1, z, :, c] = g_ref[1, z, :, c] + (g_ref[4, zd, :, c] + g_ref[7, zu, :, c])
            e_ref[2, z, :, c] = g_ref[2, z, :, c] + (g_ref[5, zd, :, c] + g_ref[8, zu, :, c])
            e_ref[3, z, :, c] = ru - rd
            p_ref[z, :, c] = density(rho)

    def out_copy(z):
        return pltpu.make_async_copy(buf.at[:, z], out_ref.at[:, z], sems.at[z])

    def second_step(z):
        zu, zd = up(z), down(z)
        left, right = [], []
        for lt in range(2):
            c = cols(lt)
            f = posts(z, lt)
            for i, plane, v in (
                (0, z, f[0]),
                (1, z, xm(f[1])),
                (2, z, xp(f[2])),
                (5, zu, f[5]),
                (6, zd, f[6]),
                (11, zu, xm(f[11])),
                (12, zd, xp(f[12])),
                (13, zd, xm(f[13])),
                (14, zu, xp(f[14])),
            ):
                buf[i, plane, :, c] = v[:rows]
            left.append([v[:rows] for v in (f[3], xm(f[7]), xp(f[10]), f[15], f[17])])
            right.append([v[:rows] for v in (f[4], xp(f[8]), xm(f[9]), f[16], f[18])])
        for n, (i, plane) in enumerate(((3, z), (7, z), (10, z), (15, zu), (17, zd))):
            v = pull_left(z, left[0][n], left[1][n], s2_ref[0, n, :rows])
            buf[i, plane, :, cols(0)], buf[i, plane, :, cols(1)] = v
        for n, (i, plane) in enumerate(((4, z), (8, z), (9, z), (16, zd), (18, zu))):
            v = pull_right(z, right[0][n], right[1][n], s2_ref[1, n, :rows])
            buf[i, plane, :, cols(0)], buf[i, plane, :, cols(1)] = v

        @pl.when(z >= 2)
        def _():
            out_copy(z - 1).start()

    gradients(0)
    loop(0, nz, first_step)
    loop(0, nz, gather)
    gradients(1)
    loop(0, nz, second_step)
    out_copy(nz - 1).start()
    out_copy(0).start()
    loop(0, nz, lambda z: out_copy(z).wait())


def body(populations):
    _, nz, rows, columns = populations.shape
    f32 = jnp.float32
    par = jnp.stack([lax.axis_index("gx") & 1, lax.axis_index("gy") & 1]).astype(jnp.int32)
    smem = pl.BlockSpec(memory_space=pltpu.SMEM)
    vmem = pl.BlockSpec(memory_space=pltpu.VMEM)
    hbm = pl.BlockSpec(memory_space=pl.ANY)
    chunks = 4
    slots = nz + 1
    edge = jax.ShapeDtypeStruct((4, slots, 8, LANES), f32)
    params = pltpu.CompilerParams(vmem_limit_bytes=40 * 1024 * 1024)

    def moments(*refs):
        moments_kernel(nz, chunks, *refs)

    m, o, sa, sb = pl.pallas_call(
        moments,
        out_shape=(
            jax.ShapeDtypeStruct((4, nz, rows, columns), f32),
            jax.ShapeDtypeStruct((4, rows, LANES), f32),
            edge,
            edge,
        ),
        in_specs=[smem, hbm],
        out_specs=(vmem, vmem, vmem, vmem),
        scratch_shapes=[
            pltpu.VMEM(populations.shape, populations.dtype),
            pltpu.SemaphoreType.DMA((chunks,)),
        ],
        compiler_params=params,
        name="moments",
    )(par, populations)
    oa = pair_swap(o, "gy", 0)
    ob = pair_swap(o, "gy", 1)
    sa, sb = pl.pallas_call(
        corner_kernel,
        out_shape=(edge, edge),
        in_specs=[smem, vmem, vmem, vmem, hbm, hbm],
        out_specs=(hbm, hbm),
        scratch_shapes=[pltpu.VMEM((2, 4, 8, LANES), f32), pltpu.SemaphoreType.DMA((2,))],
        input_output_aliases={4: 0, 5: 1},
        compiler_params=params,
        name="corners",
    )(par, o, oa, ob, sa, sb)
    ha = pair_swap(sa, "gx", 0)
    hb = pair_swap(sb, "gx", 1)

    def steps(*refs):
        step_kernel(nz, *refs)

    ring = rows + 2 * HALO
    field = (nz, ring, columns)
    return pl.pallas_call(
        steps,
        out_shape=jax.ShapeDtypeStruct((19, nz, rows, columns), f32),
        in_specs=[smem] + [vmem] * 6,
        out_specs=hbm,
        scratch_shapes=[
            pltpu.VMEM((4,) + field, f32),
            pltpu.VMEM(field, f32),
            pltpu.VMEM(field, f32),
            pltpu.VMEM(field, f32),
            pltpu.VMEM(field, f32),
            pltpu.VMEM((9,) + field, f32),
            pltpu.VMEM((4, ring, LANES), f32),
            pltpu.VMEM((2, 4, ring, LANES), f32),
            pltpu.VMEM((2, 5, ring, LANES), f32),
            pltpu.VMEM((19, nz, rows, columns), f32),
            pltpu.SemaphoreType.DMA((nz,)),
        ],
        compiler_params=params,
        name="steps",
    )(par, m, o, oa, ob, ha, hb)


def solution(mesh):
    return jax.shard_map(
        body,
        mesh=mesh,
        in_specs=(P(None, None, "gx", "gy"),),
        out_specs=P(None, None, "gx", "gy"),
        check_vma=False,
    )
```

```python
import jax
import jax.numpy as jnp
from jax import lax
from jax.experimental import pallas as pl
from jax.experimental.pallas import tpu as pltpu
from jax.sharding import PartitionSpec as P

HALO = 4
LANES = 128
STILL = (0, 3, 4, 5, 6, 15, 16, 17, 18)
RIGHT = (1, 7, 9, 11, 13)
LEFT = (2, 8, 10, 12, 14)


def pair_swap(array, axis, odd):
    size = lax.axis_size(axis)
    pairs = []
    for low in range(odd, size + odd, 2):
        a, b = low % size, (low + 1) % size
        pairs += [(a, b), (b, a)]
    return lax.ppermute(array, axis, pairs)


def iota(shape, dim):
    return lax.broadcasted_iota(jnp.int32, shape, dim)


def density(v):
    return 1.0 - jnp.exp(-v)


def loop(lo, hi, fn, unroll=4):
    count = (hi - lo) // unroll

    def group(i, c):
        for j in range(unroll):
            fn(lo + i * unroll + j)
        return c

    lax.fori_loop(0, count, group, 0)
    for left in range(lo + count * unroll, hi, 2):
        step = min(2, hi - left)
        lax.fori_loop(left, left + 1, lambda i, c: ([fn(i + j) for j in range(step)], c)[1], 0)


def moments_kernel(nz, chunks, pop_ref, rho_ref, mom_ref, o_ref, buf, sems):
    step = nz // chunks
    copies = []
    for c in range(chunks):
        part = pl.ds(c * step, step)
        copies.append(pltpu.make_async_copy(pop_ref.at[:, part], buf.at[:, part], sems.at[c]))
        copies[-1].start()
    rows = buf.shape[2]
    lane = iota((rows, LANES), 1)

    def plane(z, packed):
        tiles = []
        for lt in range(2):
            cols = slice(lt * LANES, (lt + 1) * LANES)

            def f(i):
                return buf[i, z, :, cols].astype(jnp.float32)

            rho, jx, jy, jz = f(0), None, None, None
            f1, f2 = f(1), f(2)
            rho, jx = rho + (f1 + f2), f1 - f2
            f1, f2 = f(3), f(4)
            rho, jy = rho + (f1 + f2), f1 - f2
            f1, f2 = f(5), f(6)
            rho, jz = rho + (f1 + f2), f1 - f2
            f1, f2 = f(7), f(8)
            d = f1 - f2
            rho, jx, jy = rho + (f1 + f2), jx + d, jy + d
            f1, f2 = f(9), f(10)
            d = f1 - f2
            rho, jx, jy = rho + (f1 + f2), jx + d, jy - d
            f1, f2 = f(11), f(12)
            d = f1 - f2
            rho, jx, jz = rho + (f1 + f2), jx + d, jz + d
            f1, f2 = f(13), f(14)
            d = f1 - f2
            rho, jx, jz = rho + (f1 + f2), jx + d, jz - d
            f1, f2 = f(15), f(16)
            d = f1 - f2
            rho, jy, jz = rho + (f1 + f2), jy + d, jz + d
            f1, f2 = f(17), f(18)
            d = f1 - f2
            rho, jy, jz = rho + (f1 + f2), jy + d, jz - d
            tiles.append((rho, jx, jy, jz))
        out = []
        group = nz - 1 - z
        shift = lax.rem(group * 8 + 4, LANES)
        for k in range(4):
            both = jnp.where(lane >= LANES - HALO, tiles[1][k], tiles[0][k])
            out.append(jnp.where(lane // 8 == group, pltpu.roll(both, shift, 1), packed[k]))
            for lt in range(2):
                v = tiles[lt][k]
                for x in range(0, rows, 8):
                    at = pl.ds(x * nz + z, 8, stride=nz)
                    if k == 0:
                        rho_ref[lt, at, :] = v[x : x + 8]
                    else:
                        mom_ref[k - 1, lt, at, :] = v[x : x + 8]
        return tuple(out)

    packed = (jnp.zeros((rows, LANES), jnp.float32),) * 4
    for c in range(chunks):
        copies[c].wait()

        def group(i, t, c=c):
            for j in range(4):
                t = plane(c * step + 4 * i + j, t)
            return t

        packed = lax.fori_loop(0, step // 4, group, packed)
    for k in range(4):
        o_ref[k] = packed[k]


def post_of(p, fx, fy, fz, rho, jx, jy, jz):
    inv = 1.0 / rho
    scale = p * (1.0 / 6.0)
    ux = (jx + scale * fx) * inv
    uy = (jy + scale * fy) * inv
    uz = (jz + scale * fz) * inv
    r36 = rho * (1.0 / 36.0)
    r3 = rho * (1.0 / 12.0)
    ox, oy, oz = r3 * ux, r3 * uy, r3 * uz
    hx, hy, hz = 1.5 * ux, 1.5 * uy, 1.5 * uz
    xx, yy, zz = hx * ox, hy * oy, hz * oz
    k = r36 - (xx + yy + zz) * (1.0 / 3.0)
    kx, ky, kz = k + xx, k + yy, k + zz
    out = [12.0 * k]
    for e, o in ((kx, ox), (ky, oy), (kz, oz)):
        e2, o2 = e + e, o + o
        out += [e2 + o2, e2 - o2]
    for e, a, b, h in ((kx + yy, ox, oy, hx), (kx + zz, ox, oz, hx), (ky + zz, oy, oz, hy)):
        cross = h * b
        cross = cross + cross
        ep, em = e + cross, e - cross
        op, om = a + b, a - b
        out += [ep + op, ep - op, em + om, em - om]
    return out


def strip(side, v, st_ref, s1_ref, s2_ref):
    def xp(a):
        return pltpu.roll(a, a.shape[0] - 1, 0)

    def xm(a):
        return pltpu.roll(a, 1, 0)

    def ym(a):
        return pltpu.roll(a, 1, 1)

    def yp(a):
        return pltpu.roll(a, LANES - 1, 1)

    def zm(a):
        return pltpu.roll(a, LANES - 8, 1)

    def zp(a):
        return pltpu.roll(a, 8, 1)

    def post(p, v):
        a, b = ym(p), yp(p)
        q, d = p + p + (a + b), b - a
        bb = q + (xp(p) + xm(p))
        aa = q + (zp(p) + zm(p))
        fx = xp(aa) - xm(aa)
        fy = d + d + (xp(d) + xm(d)) + (zp(d) + zm(d))
        fz = zp(bb) - zm(bb)
        return post_of(p, fx, fy, fz, *v)

    p = density(v[0])
    st_ref[side] = p
    f = post(p, v)
    a15, a17, a18, a16 = zm(f[15]), zp(f[17]), zm(f[18]), zp(f[16])
    sp, jp = f[3] + (a15 + a17), a15 - a17
    sn, jn = f[4] + (a18 + a16), a18 - a16
    for n, w in enumerate((sp, jp, f[7], f[10]) if side == 0 else (sn, jn, f[9], f[8])):
        s1_ref[side, n] = w
    sp, jp, sn, jn = ym(sp), ym(jp), yp(sn), yp(jn)
    a, b = zm(f[5]), zp(f[6])
    r0, jz0, jy0 = f[0] + (a + b) + (sp + sn), (a - b) + (jp + jn), sp - sn
    a, b, c, e = ym(f[7]), yp(f[9]), zm(f[11]), zp(f[13])
    ru, jyu, jzu = xm(f[1] + (a + b) + (c + e)), xm(a - b), xm(c - e)
    a, b, c, e = ym(f[10]), yp(f[8]), zm(f[14]), zp(f[12])
    rd, jyd, jzd = xp(f[2] + (a + b) + (c + e)), xp(a - b), xp(c - e)
    v = (r0 + (ru + rd), ru - rd, jy0 + (jyu + jyd), jz0 + (jzu + jzd))
    p = density(v[0])
    st_ref[2 + side] = p
    f = post(p, v)
    if side == 0:
        keep = (f[3], zm(f[15]), zp(f[17]), f[7], f[10])
    else:
        keep = (f[4], zp(f[16]), zm(f[18]), f[8], f[9])
    for n, w in enumerate(keep):
        s2_ref[side, n] = w


class Rows:
    def __init__(self, nz):
        self.nz = nz
        lane = iota((nz, LANES), 1)
        self.first, self.last = lane == 0, lane == LANES - 1

    def at(self, x):
        return pl.ds(pl.multiple_of(x * self.nz, self.nz), self.nz)

    def zp(self, v):
        return pltpu.roll(v, self.nz - 1, 0)

    def zm(self, v):
        return pltpu.roll(v, 1, 0)

    def edge(self, row, shift):
        wide = jnp.broadcast_to(row, (8, LANES))
        return jnp.concatenate(
            [pltpu.roll(wide, shift + 8 * z, 1, stride=8, stride_axis=0) for z in range(0, self.nz, 8)],
            axis=0,
        )

    def ym(self, a, row):
        r0, r1 = pltpu.roll(a[0], 1, 1), pltpu.roll(a[1], 1, 1)
        h = self.edge(row, 5)
        return jnp.where(self.first, h, r0), jnp.where(self.first, r0, r1)

    def yp(self, a, row):
        r0, r1 = pltpu.roll(a[0], LANES - 1, 1), pltpu.roll(a[1], LANES - 1, 1)
        h = self.edge(row, 3)
        return jnp.where(self.last, r1, r0), jnp.where(self.last, h, r1)

    def plane(self, x, p, left, right, w_ref):
        a, b = self.ym(p, left), self.yp(p, right)
        for lt in range(2):
            q = p[lt] + p[lt] + (a[lt] + b[lt])
            w_ref[0, lt, self.at(x), :] = p[lt]
            w_ref[1, lt, self.at(x), :] = q
            w_ref[2, lt, self.at(x), :] = q + (self.zp(p[lt]) + self.zm(p[lt]))
            w_ref[3, lt, self.at(x), :] = b[lt] - a[lt]

    def posts(self, x, lt, w_ref, v):
        u, n, d = self.at(x + 1), self.at(x), self.at(x - 1)
        p = w_ref[0, lt, n, :]
        bb = w_ref[1, lt, n, :] + (w_ref[0, lt, u, :] + w_ref[0, lt, d, :])
        dd = w_ref[3, lt, n, :]
        fx = w_ref[2, lt, u, :] - w_ref[2, lt, d, :]
        fy = dd + dd + (self.zp(dd) + self.zm(dd)) + (w_ref[3, lt, u, :] + w_ref[3, lt, d, :])
        fz = self.zp(bb) - self.zm(bb)
        return post_of(p, fx, fy, fz, *v)

    def first_step(self, x, w_ref, v, g_ref, s1):
        zp, zm = self.zp, self.zm
        part, left, right = [], [], []
        for lt in range(2):
            f = self.posts(x, lt, w_ref, [v(k, lt) for k in range(4)])
            a15, a17, a18, a16 = zm(f[15]), zp(f[17]), zm(f[18]), zp(f[16])
            left.append((f[3] + (a15 + a17), a15 - a17, f[7], f[10]))
            right.append((f[4] + (a18 + a16), a18 - a16, f[9], f[8]))
            a, b = zm(f[5]), zp(f[6])
            s = [f[0] + (a + b), a - b]
            a, b = zm(f[11]), zp(f[13])
            s += [f[1] + (a + b), a - b]
            a, b = zm(f[14]), zp(f[12])
            s += [f[2] + (a + b), a - b]
            part.append(s)
        m = [self.ym((left[0][n], left[1][n]), s1(0, n)) for n in range(4)]
        q = [self.yp((right[0][n], right[1][n]), s1(1, n)) for n in range(4)]
        for lt in range(2):
            s = part[lt]

            def put(n, value):
                g_ref[n, lt, self.at(x), :] = value

            put(0, s[0] + (m[0][lt] + q[0][lt]))
            put(1, m[0][lt] - q[0][lt])
            put(2, s[1] + (m[1][lt] + q[1][lt]))
            put(3, s[2] + (m[2][lt] + q[2][lt]))
            put(4, m[2][lt] - q[2][lt])
            put(5, s[3])
            put(6, s[4] + (m[3][lt] + q[3][lt]))
            put(7, m[3][lt] - q[3][lt])
            put(8, s[5])

    def gather(self, x, g_ref, e_ref):
        u, n, d = self.at(x + 1), self.at(x), self.at(x - 1)
        p = []
        for lt in range(2):
            ru, rd = g_ref[3, lt, d, :], g_ref[6, lt, u, :]
            rho = g_ref[0, lt, n, :] + (ru + rd)
            e_ref[0, lt, n, :] = rho
            e_ref[1, lt, n, :] = ru - rd
            for k in (1, 2):
                e_ref[k + 1, lt, n, :] = g_ref[k, lt, n, :] + (
                    g_ref[k + 3, lt, d, :] + g_ref[k + 6, lt, u, :]
                )
            p.append(density(rho))
        return p

    def second_step(self, x, w_ref, e_ref, s2, buf, shift):
        zp, zm = self.zp, self.zm
        left, right = [], []
        n, u, d = x + shift, x + shift + 1, x + shift - 1

        def put(i, row, lt, v):
            buf[row, i, :, lt * LANES : (lt + 1) * LANES] = v

        for lt in range(2):
            f = self.posts(x, lt, w_ref, [e_ref[k, lt, self.at(x), :] for k in range(4)])
            put(0, n, lt, f[0])
            put(5, n, lt, zm(f[5]))
            put(6, n, lt, zp(f[6]))
            put(1, u, lt, f[1])
            put(11, u, lt, zm(f[11]))
            put(13, u, lt, zp(f[13]))
            put(2, d, lt, f[2])
            put(12, d, lt, zp(f[12]))
            put(14, d, lt, zm(f[14]))
            left.append((f[3], zm(f[15]), zp(f[17]), f[7], f[10]))
            right.append((f[4], zp(f[16]), zm(f[18]), f[8], f[9]))
        for j, (i, row) in enumerate(((3, n), (15, n), (17, n), (7, u), (10, d))):
            v = self.ym((left[0][j], left[1][j]), s2(0, j))
            put(i, row, 0, v[0])
            put(i, row, 1, v[1])
        for j, (i, row) in enumerate(((4, n), (16, n), (18, n), (8, d), (9, u))):
            v = self.yp((right[0][j], right[1][j]), s2(1, j))
            put(i, row, 0, v[0])
            put(i, row, 1, v[1])


def inner_kernel(nz, rows, rho_ref, mom_ref, t_ref, buf, w0_ref, g_ref, e_ref, w1_ref,
                 st_ref, s1_ref, s2_ref):
    r = Rows(nz)
    for side in range(2):
        strip(side, [t_ref[side, k] for k in range(4)], st_ref, s1_ref, s2_ref)

    def row(ref, *at):
        return ref[at[:-1] + (pl.ds(at[-1], 1), slice(None))]

    def start(x):
        p = [density(rho_ref[lt, r.at(x), :]) for lt in range(2)]
        r.plane(x, p, row(st_ref, 0, x), row(st_ref, 1, x), w0_ref)

    def first(x):
        def v(k, lt):
            return rho_ref[lt, r.at(x), :] if k == 0 else mom_ref[k - 1, lt, r.at(x), :]

        r.first_step(x, w0_ref, v, g_ref, lambda side, n: row(s1_ref, side, n, x))

    def middle(x):
        p = r.gather(x, g_ref, e_ref)
        r.plane(x, p, row(st_ref, 2, x), row(st_ref, 3, x), w1_ref)

    def second(x):
        r.second_step(x, w1_ref, e_ref, lambda side, n: row(s2_ref, side, n, x), buf, -2)

    loop(0, rows, start)
    loop(1, rows - 1, first)
    loop(2, rows - 2, middle)
    loop(3, rows - 3, second)


def outer_kernel(nz, rows, rho_ref, mom_ref, t_ref, hl_ref, hr_ref, w0_in, g_in, e_in, w1_in, buf_in,
                 out_ref, e0_ref, w0_ref, g_ref, e_ref, w1_ref, st_ref, s1_ref, s2_ref, buf, sems):
    r = Rows(nz)

    def send(source, x):
        return pltpu.make_async_copy(source, out_ref.at[:, :, x, :], sems.at[x])

    inside = [send(buf_in.at[x - 2], x) for x in range(HALO, rows - HALO)]
    for copy in inside:
        copy.start()
    block = 2 * nz
    rho_rows = HALO * block
    mom_rows = (HALO - 1) * block

    def halo_rho(ref, j, lt):
        return ref[pl.ds((lt * HALO + j) * nz, nz), :]

    def halo_mom(ref, k, j, lt):
        return ref[pl.ds(rho_rows + k * mom_rows + (lt * (HALO - 1) + j) * nz, nz), :]

    for side in range(2):
        v = []
        base = rho_rows + 3 * mom_rows
        for k in range(4):
            hl = hl_ref[pl.ds(base + 8 * k, 8), :]
            hr = hr_ref[pl.ds(base + 8 * k, 8), :]
            low = iota((8, LANES), 0) < HALO
            if side == 0:
                tile = jnp.where(low, hr, pltpu.roll(hl, HALO, 0))
            else:
                tile = jnp.where(low, pltpu.roll(hr, HALO, 0), hl)
            v.append(jnp.concatenate([t_ref[side, k], tile], axis=0))
        strip(side, v, st_ref, s1_ref, s2_ref)

    ring = rows + 2 * HALO

    def ring_of(l):
        x = jnp.where(l < 10, l - HALO, l - 10 + rows - 6)
        return jnp.where(x < 0, x + ring, x)

    def row(ref, *at):
        return ref[at[:-1] + (pl.ds(ring_of(at[-1]), 1), slice(None))]

    def move(dst, src, field, l, x):
        for lt in range(2):
            dst[field, lt, r.at(l), :] = src[field, lt, r.at(x), :]

    def rho_mom(dst, x):
        for lt in range(2):
            e0_ref[0, lt, r.at(dst), :] = rho_ref[lt, r.at(x), :]
            for k in range(3):
                e0_ref[k + 1, lt, r.at(dst), :] = mom_ref[k, lt, r.at(x), :]

    rho_mom(3, 0)
    rho_mom(4, rows - 1)
    for lt in range(2):
        for j in range(3):
            e0_ref[0, lt, r.at(j), :] = halo_rho(hl_ref, j + 1, lt)
            e0_ref[0, lt, r.at(5 + j), :] = halo_rho(hr_ref, j, lt)
            for k in range(3):
                e0_ref[k + 1, lt, r.at(j), :] = halo_mom(hl_ref, k, j, lt)
                e0_ref[k + 1, lt, r.at(5 + j), :] = halo_mom(hr_ref, k, j, lt)
    for field in range(4):
        for l, x in ((4, 0), (5, 1), (14, rows - 2), (15, rows - 1)):
            move(w0_ref, w0_in, field, l, x)
        for l, x in ((6, 2), (7, 3), (12, rows - 4), (13, rows - 3)):
            move(w1_ref, w1_in, field, l, x)
        move(e_ref, e_in, field, 6, 2)
        move(e_ref, e_in, field, 13, rows - 3)
    for field in range(3):
        move(g_ref, g_in, field, 5, 1)
        move(g_ref, g_in, field, 14, rows - 2)
        for l, x in ((5, 1), (6, 2)):
            move(g_ref, g_in, 6 + field, l, x)
        for l, x in ((13, rows - 3), (14, rows - 2)):
            move(g_ref, g_in, 3 + field, l, x)

    def start(n):
        side, j = n >> 2, n & 3
        l = jnp.where(side == 0, j, 16 + j)
        p = []
        for lt in range(2):
            at = pl.ds(pl.multiple_of((lt * HALO + j) * nz, nz), nz)
            p.append(density(jnp.where(side == 0, hl_ref[at, :], hr_ref[at, :])))
        r.plane(l, p, row(st_ref, 0, l), row(st_ref, 1, l), w0_ref)

    def first(n):
        l = jnp.where(n < 4, n + 1, n + 11)
        r.first_step(
            l, w0_ref, lambda k, lt: e0_ref[k, lt, r.at(n), :], g_ref,
            lambda side, m: row(s1_ref, side, m, l),
        )

    def middle(n):
        l = jnp.where(n < 4, n + 2, n + 10)
        p = r.gather(l, g_ref, e_ref)
        r.plane(l, p, row(st_ref, 2, l), row(st_ref, 3, l), w1_ref)

    def second(n):
        l = jnp.where(n < 4, n + 3, n + 9)
        r.second_step(l, w1_ref, e_ref, lambda side, m: row(s2_ref, side, m, l), buf, 0)

    for l, x, indices in (
        (6, 2, LEFT),
        (7, 3, STILL + LEFT),
        (12, rows - 4, STILL + RIGHT),
        (13, rows - 3, RIGHT),
    ):
        for i in indices:
            buf[l, i] = buf_in[x - 2, i]

    loop(0, 8, start, 8)
    loop(0, 8, first, 8)
    loop(0, 8, middle, 8)
    loop(0, 4, second)
    edges = [send(buf.at[x + HALO], x) for x in range(HALO)]
    for copy in edges:
        copy.start()
    loop(4, 8, second)
    edges += [send(buf.at[x + 16 - rows], x) for x in range(rows - HALO, rows)]
    for copy in edges[HALO:]:
        copy.start()
    for copy in inside + edges:
        copy.wait()


def body(populations):
    _, nz, rows, columns = populations.shape
    f32 = jnp.float32
    even_x = (lax.axis_index("gx") & 1) == 0
    even_y = (lax.axis_index("gy") & 1) == 0
    vmem = pl.BlockSpec(memory_space=pltpu.VMEM)
    hbm = pl.BlockSpec(memory_space=pltpu.HBM)
    chunks = 4
    params = pltpu.CompilerParams(vmem_limit_bytes=40 * 1024 * 1024)

    def shape(*dims):
        return jax.ShapeDtypeStruct(dims, f32)

    def field(n, count):
        return (n, 2, count * nz, LANES)

    def moments(*refs):
        moments_kernel(nz, chunks, *refs)

    rho, mom, o = pl.pallas_call(
        moments,
        out_shape=(shape(2, rows * nz, LANES), shape(*field(3, rows)), shape(4, rows, LANES)),
        in_specs=[hbm],
        out_specs=(vmem, vmem, vmem),
        scratch_shapes=[
            pltpu.VMEM(populations.shape, populations.dtype),
            pltpu.SemaphoreType.DMA((chunks,)),
        ],
        compiler_params=pltpu.CompilerParams(vmem_limit_bytes=50 * 1024 * 1024),
        name="moments",
    )(pltpu.with_memory_space_constraint(populations, pltpu.HBM))

    oa = pair_swap(o, "gy", 0)
    ob = pair_swap(o, "gy", 1)
    own = (iota(o.shape, 2) & 7) < HALO
    right, left = jnp.where(even_y, oa, ob), jnp.where(even_y, ob, oa)
    sides = jnp.stack([jnp.where(own, left, o), jnp.where(own, o, right)])

    def edge(low):
        a = slice(0, HALO * nz) if low else slice((rows - HALO) * nz, rows * nz)
        b = slice(0, (HALO - 1) * nz) if low else slice((rows - HALO + 1) * nz, rows * nz)
        c = slice(0, HALO) if low else slice(rows - HALO, rows)
        return jnp.concatenate([
            rho[:, a].reshape(-1, LANES),
            mom[:, :, b].reshape(-1, LANES),
            jnp.concatenate([sides[0, :, c], sides[1, :, c]], axis=1).reshape(-1, LANES),
        ])

    low, high = edge(True), edge(False)
    ha = pair_swap(jnp.where(even_x, high, low), "gx", 0)
    hb = pair_swap(jnp.where(even_x, low, high), "gx", 1)

    def inner(*refs):
        inner_kernel(nz, rows, *refs)

    buf, w0, g, e, w1 = pl.pallas_call(
        inner,
        out_shape=(
            shape(rows - HALO, 19, nz, columns), shape(*field(4, rows)), shape(*field(9, rows)),
            shape(*field(4, rows)), shape(*field(4, rows)),
        ),
        in_specs=[vmem, vmem, vmem],
        out_specs=(vmem, vmem, vmem, vmem, vmem),
        scratch_shapes=[
            pltpu.VMEM((4, rows, LANES), f32),
            pltpu.VMEM((2, 4, rows, LANES), f32),
            pltpu.VMEM((2, 5, rows, LANES), f32),
        ],
        compiler_params=params,
        cost_estimate=pl.CostEstimate(flops=20_000_000, bytes_accessed=2_500_000, transcendentals=0),
        name="inner",
    )(rho, mom, sides)
    hl, hr = jnp.where(even_x, hb, ha), jnp.where(even_x, ha, hb)

    def outer(*refs):
        outer_kernel(nz, rows, *refs)

    ring = rows + 2 * HALO
    return pl.pallas_call(
        outer,
        out_shape=shape(*populations.shape),
        in_specs=[vmem] * 10,
        out_specs=hbm,
        scratch_shapes=[
            pltpu.VMEM(field(4, 8), f32),
            pltpu.VMEM(field(4, 20), f32),
            pltpu.VMEM(field(9, 20), f32),
            pltpu.VMEM(field(4, 20), f32),
            pltpu.VMEM(field(4, 20), f32),
            pltpu.VMEM((4, ring, LANES), f32),
            pltpu.VMEM((2, 4, ring, LANES), f32),
            pltpu.VMEM((2, 5, ring, LANES), f32),
            pltpu.VMEM((20, 19, nz, columns), f32),
            pltpu.SemaphoreType.DMA((rows,)),
        ],
        compiler_params=params,
        name="outer",
    )(rho, mom, sides, hl, hr, w0, g, e, w1, buf)


def solution(mesh):
    return jax.shard_map(
        body,
        mesh=mesh,
        in_specs=(P(None, None, "gx", "gy"),),
        out_specs=P(None, None, "gx", "gy"),
        check_vma=False,
    )
```

```python
import jax
import jax.numpy as jnp
from jax import lax
from jax.experimental import pallas as pl
from jax.experimental.pallas import tpu as pltpu
from jax.sharding import PartitionSpec as P

HALO = 4
LANES = 128
STILL = (0, 3, 4, 5, 6, 15, 16, 17, 18)
RIGHT = (1, 7, 9, 11, 13)
LEFT = (2, 8, 10, 12, 14)


def pair_swap(array, axis, odd):
    size = lax.axis_size(axis)
    pairs = []
    for low in range(odd, size + odd, 2):
        a, b = low % size, (low + 1) % size
        pairs += [(a, b), (b, a)]
    return lax.ppermute(array, axis, pairs)


def iota(shape, dim):
    return lax.broadcasted_iota(jnp.int32, shape, dim)


def density(v):
    return 1.0 - jnp.exp(-v)


def loop(lo, hi, fn, unroll=4):
    count = (hi - lo) // unroll

    def group(i, c):
        for j in range(unroll):
            fn(lo + i * unroll + j)
        return c

    lax.fori_loop(0, count, group, 0)
    for left in range(lo + count * unroll, hi, 2):
        step = min(2, hi - left)
        lax.fori_loop(left, left + 1, lambda i, c: ([fn(i + j) for j in range(step)], c)[1], 0)


def moments_kernel(nz, chunks, pop_ref, rho_ref, mom_ref, o_ref, l_ref, r_ref, buf, sems):
    step = nz // chunks
    copies = []
    for c in range(chunks):
        part = pl.ds(c * step, step)
        copies.append(pltpu.make_async_copy(pop_ref.at[:, part], buf.at[:, part], sems.at[c]))
        copies[-1].start()
    rows = buf.shape[2]
    lane = iota((rows, LANES), 1)

    def plane(z, packed):
        tiles = []
        for lt in range(2):
            cols = slice(lt * LANES, (lt + 1) * LANES)

            def f(i):
                return buf[i, z, :, cols].astype(jnp.float32)

            rho, jx, jy, jz = f(0), None, None, None
            f1, f2 = f(1), f(2)
            rho, jx = rho + (f1 + f2), f1 - f2
            f1, f2 = f(3), f(4)
            rho, jy = rho + (f1 + f2), f1 - f2
            f1, f2 = f(5), f(6)
            rho, jz = rho + (f1 + f2), f1 - f2
            f1, f2 = f(7), f(8)
            d = f1 - f2
            rho, jx, jy = rho + (f1 + f2), jx + d, jy + d
            f1, f2 = f(9), f(10)
            d = f1 - f2
            rho, jx, jy = rho + (f1 + f2), jx + d, jy - d
            f1, f2 = f(11), f(12)
            d = f1 - f2
            rho, jx, jz = rho + (f1 + f2), jx + d, jz + d
            f1, f2 = f(13), f(14)
            d = f1 - f2
            rho, jx, jz = rho + (f1 + f2), jx + d, jz - d
            f1, f2 = f(15), f(16)
            d = f1 - f2
            rho, jy, jz = rho + (f1 + f2), jy + d, jz + d
            f1, f2 = f(17), f(18)
            d = f1 - f2
            rho, jy, jz = rho + (f1 + f2), jy + d, jz - d
            tiles.append((rho, jx, jy, jz))
        out = []
        group = nz - 1 - z
        shift = lax.rem(group * 8 + 4, LANES)
        for k in range(4):
            both = jnp.where(lane >= LANES - HALO, tiles[1][k], tiles[0][k])
            out.append(jnp.where(lane // 8 == group, pltpu.roll(both, shift, 1), packed[k]))
            for lt in range(2):
                v = tiles[lt][k]
                for x in range(0, rows, 8):
                    at = pl.ds(x * nz + z, 8, stride=nz)
                    if k == 0:
                        rho_ref[lt, at, :] = v[x : x + 8]
                    else:
                        mom_ref[k - 1, lt, at, :] = v[x : x + 8]
        return tuple(out)

    packed = (jnp.zeros((rows, LANES), jnp.float32),) * 4
    for c in range(chunks):
        copies[c].wait()

        def group(i, t, c=c):
            for j in range(4):
                t = plane(c * step + 4 * i + j, t)
            return t

        packed = lax.fori_loop(0, step // 4, group, packed)
    for k in range(4):
        o_ref[k] = packed[k]
    high = (lane & 7) < HALO
    for n in range(2):
        a, b = packed[2 * n : 2 * n + 2]
        l_ref[n] = jnp.where(high, pltpu.roll(b, LANES - HALO, 1), a)
        r_ref[n] = jnp.where(high, a, pltpu.roll(b, HALO, 1))


def strips_of(o, left, right):
    own = (iota(o[0].shape, 1) & 7) < HALO
    ls, rs = [], []
    for n in range(2):
        a, b = o[2 * n : 2 * n + 2]
        ls += [jnp.where(own, left[n], a), jnp.where(own, pltpu.roll(left[n], LANES - HALO, 1), b)]
        rs += [jnp.where(own, a, right[n]), jnp.where(own, b, pltpu.roll(right[n], HALO, 1))]
    return ls, rs


def pushed(p, force, momentum):
    scale = p * (1.0 / 6.0)
    return [j + scale * f for j, f in zip(momentum, force)]


def post_of(rho, momentum):
    inv = 1.0 / rho
    ux, uy, uz = [j * inv for j in momentum]
    r36 = rho * (1.0 / 36.0)
    r3 = rho * (1.0 / 12.0)
    ox, oy, oz = r3 * ux, r3 * uy, r3 * uz
    hx, hy, hz = 1.5 * ux, 1.5 * uy, 1.5 * uz
    xx, yy, zz = hx * ox, hy * oy, hz * oz
    k = r36 - (xx + yy + zz) * (1.0 / 3.0)
    kx, ky, kz = k + xx, k + yy, k + zz
    out = [12.0 * k]
    for e, o in ((kx, ox), (ky, oy), (kz, oz)):
        e2, o2 = e + e, o + o
        out += [e2 + o2, e2 - o2]
    for e, a, b, h in ((kx + yy, ox, oy, hx), (kx + zz, ox, oz, hx), (ky + zz, oy, oz, hy)):
        cross = h * b
        cross = cross + cross
        ep, em = e + cross, e - cross
        op, om = a + b, a - b
        out += [ep + op, ep - op, em + om, em - om]
    return out


def strips_of_step(strips, s_ref):
    def xp(a):
        return pltpu.roll(a, a.shape[0] - 1, 0)

    def xm(a):
        return pltpu.roll(a, 1, 0)

    def ym(a):
        return pltpu.roll(a, 1, 1)

    def yp(a):
        return pltpu.roll(a, LANES - 1, 1)

    def zm(a):
        return pltpu.roll(a, LANES - 8, 1)

    def zp(a):
        return pltpu.roll(a, 8, 1)

    def post(p, v):
        a, b = ym(p), yp(p)
        q, d = p + p + (a + b), b - a
        bb = q + (xp(p) + xm(p))
        aa = q + (zp(p) + zm(p))
        fx = xp(aa) - xm(aa)
        fy = d + d + (xp(d) + xm(d)) + (zp(d) + zm(d))
        fz = zp(bb) - zm(bb)
        return post_of(v[0], pushed(p, (fx, fy, fz), v[1:]))

    own = (iota(strips[0][0].shape, 1) & 7) < HALO
    moments, later = [], []
    for side, v in enumerate(strips):
        f = post(density(v[0]), v)
        a15, a17, a18, a16 = zm(f[15]), zp(f[17]), zm(f[18]), zp(f[16])
        sp, jp = ym(f[3] + (a15 + a17)), ym(a15 - a17)
        sn, jn = yp(f[4] + (a18 + a16)), yp(a18 - a16)
        a, b = zm(f[5]), zp(f[6])
        r0, jz0, jy0 = f[0] + (a + b) + (sp + sn), (a - b) + (jp + jn), sp - sn
        a, b, c, e = ym(f[7]), yp(f[9]), zm(f[11]), zp(f[13])
        ru, jyu, jzu = xm(f[1] + (a + b) + (c + e)), xm(a - b), xm(c - e)
        a, b, c, e = ym(f[10]), yp(f[8]), zm(f[14]), zp(f[12])
        rd, jyd, jzd = xp(f[2] + (a + b) + (c + e)), xp(a - b), xp(c - e)
        v = (r0 + (ru + rd), ru - rd, jy0 + (jyu + jyd), jz0 + (jzu + jzd))
        moments.append(v)
        p = density(v[0])
        f = post(p, v)
        if side == 0:
            later.append((p, f[3], zm(f[15]), zp(f[17]), f[7], f[10]))
        else:
            later.append((p, f[4], zp(f[16]), zm(f[18]), f[8], f[9]))
    for k in range(4):
        s_ref[k] = jnp.where(own, moments[1][k], moments[0][k])
    lane = iota(own.shape, 1) & 7
    for n in range(6):
        s_ref[4 + n] = jnp.where(lane == HALO - 1, later[0][n], pltpu.roll(later[1][n], LANES - 2, 1))


class Rows:
    def __init__(self, nz):
        self.nz = nz
        lane = iota((nz, LANES), 1)
        self.first, self.last = lane == 0, lane == LANES - 1
        self.two = lane < 2, lane >= LANES - 2

    def at(self, x):
        if isinstance(x, int):
            return pl.ds(x * self.nz, self.nz)
        return pl.ds(pl.multiple_of(x * self.nz, self.nz), self.nz)

    def of(self, ref):
        return lambda n, lt, x: ref[n, lt, self.at(x), :]

    def zp(self, v):
        return pltpu.roll(v, self.nz - 1, 0)

    def zm(self, v):
        return pltpu.roll(v, 1, 0)

    def edge(self, row, shift):
        wide = jnp.broadcast_to(row, (8, LANES))
        return jnp.concatenate(
            [pltpu.roll(wide, shift + 8 * z, 1, stride=8, stride_axis=0) for z in range(0, self.nz, 8)],
            axis=0,
        )

    def ym(self, a, h=None):
        r0, r1 = pltpu.roll(a[0], 1, 1), pltpu.roll(a[1], 1, 1)
        return r0 if h is None else jnp.where(self.first, h, r0), jnp.where(self.first, r0, r1)

    def yp(self, a, h=None):
        r0, r1 = pltpu.roll(a[0], LANES - 1, 1), pltpu.roll(a[1], LANES - 1, 1)
        return jnp.where(self.last, r1, r0), r1 if h is None else jnp.where(self.last, h, r1)

    def plane(self, x, p, w_ref, row=None):
        h = None if row is None else self.edge(row, 5)
        a, b = self.ym(p, h), self.yp(p, h)
        for lt in range(2):
            q = p[lt] + p[lt] + (a[lt] + b[lt])
            w_ref[0, lt, self.at(x), :] = p[lt]
            w_ref[1, lt, self.at(x), :] = q
            w_ref[2, lt, self.at(x), :] = q + (self.zp(p[lt]) + self.zm(p[lt]))
            w_ref[3, lt, self.at(x), :] = b[lt] - a[lt]

    def posts(self, x, lt, w, v):
        bb = w(1, lt, x) + (w(0, lt, x + 1) + w(0, lt, x - 1))
        dd = w(3, lt, x)
        fx = w(2, lt, x + 1) - w(2, lt, x - 1)
        fy = dd + dd + (self.zp(dd) + self.zm(dd)) + (w(3, lt, x + 1) + w(3, lt, x - 1))
        fz = self.zp(bb) - self.zm(bb)
        m = pushed(w(0, lt, x), (fx, fy, fz), [v(k, lt, x) for k in (1, 2, 3)])
        return post_of(v(0, lt, x), m)

    def half(self, x, other, lt, w, v):
        bb = w(1, lt, x) + w(0, lt, other)
        dd = w(3, lt, x)
        fx = w(2, lt, other) if other > x else -w(2, lt, other)
        fy = dd + dd + (self.zp(dd) + self.zm(dd)) + w(3, lt, other)
        fz = self.zp(bb) - self.zm(bb)
        return pushed(w(0, lt, x), (fx, fy, fz), [v(k, lt, x) for k in (1, 2, 3)])

    def rest(self, x, other, lt, w, v):
        p = w(0, lt, other)
        fx = w(2, lt, other) if other > x else -w(2, lt, other)
        fz = self.zp(p) - self.zm(p)
        m = pushed(w(0, lt, x), (fx, w(3, lt, other), fz), [v(k, lt, x) for k in (1, 2, 3)])
        return post_of(v(0, lt, x), m)

    def first_step(self, x, g_ref, posts):
        zp, zm = self.zp, self.zm
        part, left, right = [], [], []
        for lt in range(2):
            f = posts(lt)
            a15, a17, a18, a16 = zm(f[15]), zp(f[17]), zm(f[18]), zp(f[16])
            left.append((f[3] + (a15 + a17), a15 - a17, f[7], f[10]))
            right.append((f[4] + (a18 + a16), a18 - a16, f[9], f[8]))
            a, b = zm(f[5]), zp(f[6])
            s = [f[0] + (a + b), a - b]
            a, b = zm(f[11]), zp(f[13])
            s += [f[1] + (a + b), a - b]
            a, b = zm(f[14]), zp(f[12])
            s += [f[2] + (a + b), a - b]
            part.append(s)
        m = [self.ym((left[0][n], left[1][n])) for n in range(4)]
        q = [self.yp((right[0][n], right[1][n])) for n in range(4)]
        for lt in range(2):
            s = part[lt]

            def put(n, value):
                g_ref[n, lt, self.at(x), :] = value

            put(0, s[0] + (m[0][lt] + q[0][lt]))
            put(1, m[0][lt] - q[0][lt])
            put(2, s[1] + (m[1][lt] + q[1][lt]))
            put(3, s[2] + (m[2][lt] + q[2][lt]))
            put(4, m[2][lt] - q[2][lt])
            put(5, s[3])
            put(6, s[4] + (m[3][lt] + q[3][lt]))
            put(7, m[3][lt] - q[3][lt])
            put(8, s[5])

    def gather(self, x, g):
        out = []
        for lt in range(2):
            ru, rd = g(3, lt, x - 1), g(6, lt, x + 1)
            v = [g(0, lt, x) + (ru + rd), ru - rd]
            for k in (1, 2):
                v.append(g(k, lt, x) + (g(k + 3, lt, x - 1) + g(k + 6, lt, x + 1)))
            out.append(v)
        return out

    def patch(self, x, v, row, e_ref):
        for k in range(len(v[0])):
            h = self.edge(row(k), 4)
            v[0][k] = jnp.where(self.two[0], h, v[0][k])
            v[1][k] = jnp.where(self.two[1], h, v[1][k])
            for lt in range(2):
                e_ref[k, lt, self.at(x), :] = v[lt][k]
        return [density(v[0][0]), density(v[1][0])]

    def second_step(self, x, w, e, row, buf, shift):
        zp, zm = self.zp, self.zm
        left, right = [], []
        n, u, d = x + shift, x + shift + 1, x + shift - 1

        def put(i, row, lt, v):
            buf[row, i, :, lt * LANES : (lt + 1) * LANES] = v

        for lt in range(2):
            f = self.posts(x, lt, w, e)
            put(0, n, lt, f[0])
            put(5, n, lt, zm(f[5]))
            put(6, n, lt, zp(f[6]))
            put(1, u, lt, f[1])
            put(11, u, lt, zm(f[11]))
            put(13, u, lt, zp(f[13]))
            put(2, d, lt, f[2])
            put(12, d, lt, zp(f[12]))
            put(14, d, lt, zm(f[14]))
            left.append((f[3], zm(f[15]), zp(f[17]), f[7], f[10]))
            right.append((f[4], zp(f[16]), zm(f[18]), f[8], f[9]))
        h = [self.edge(row(5 + j), 5) for j in range(5)]
        for j, (i, to) in enumerate(((3, n), (15, n), (17, n), (7, u), (10, d))):
            v = self.ym((left[0][j], left[1][j]), h[j])
            put(i, to, 0, v[0])
            put(i, to, 1, v[1])
        for j, (i, to) in enumerate(((4, n), (16, n), (18, n), (8, d), (9, u))):
            v = self.yp((right[0][j], right[1][j]), h[j])
            put(i, to, 0, v[0])
            put(i, to, 1, v[1])


def early_kernel(nz, rows, rho_ref, mom_ref, w_ref, g_ref, e_ref, x_ref):
    r = Rows(nz)
    w, g = r.of(w_ref), r.of(g_ref)

    def v(k, lt, x):
        return rho_ref[lt, r.at(x), :] if k == 0 else mom_ref[k - 1, lt, r.at(x), :]

    def start(x):
        r.plane(x, [density(rho_ref[lt, r.at(x), :]) for lt in range(2)], w_ref)

    def first(x):
        r.first_step(x, g_ref, lambda lt: r.posts(x, lt, w, v))

    def middle(x):
        v = r.gather(x, g)
        for lt in range(2):
            for k in range(4):
                e_ref[k, lt, r.at(x), :] = v[lt][k]

    loop(0, rows, start)
    for side, x, other in ((0, 0, 1), (1, rows - 1, rows - 2)):
        for lt in range(2):
            x_ref[side, r.at(8 + lt), :] = v(0, lt, x)
            for k, j in enumerate(r.half(x, other, lt, w, v)):
                x_ref[side, r.at(10 + 2 * k + lt), :] = j
    loop(1, rows - 1, first)
    loop(2, rows - 2, middle)
    for side, base, x, other in ((0, 6, 1, 2), (1, 3, rows - 2, rows - 3)):
        for lt in range(2):
            x_ref[side, r.at(lt), :] = g(0, lt, x) + g(base, lt, other)
            for k in range(3):
                x_ref[side, r.at(2 + 2 * k + lt), :] = g(base + k, lt, x)


def inner_kernel(nz, rows, e_in, o_ref, l_ref, r_ref, buf, e_ref, w_ref, s_ref):
    r = Rows(nz)
    strips_of_step(
        strips_of(
            [o_ref[k] for k in range(4)], [l_ref[k] for k in range(2)], [r_ref[k] for k in range(2)]
        ),
        s_ref,
    )

    def row(x):
        return lambda n: s_ref[n, pl.ds(x, 1), :]

    def middle(x):
        v = [[e_in[k, lt, r.at(x), :] for k in range(4)] for lt in range(2)]
        p = r.patch(x, v, row(x), e_ref)
        r.plane(x, p, w_ref, row(x)(4))

    def second(x):
        r.second_step(x, r.of(w_ref), r.of(e_ref), row(x), buf, -2)

    loop(2, rows - 2, middle)
    loop(3, rows - 3, second)


def outer_kernel(nz, rows, x_ref, o_ref, l_ref, r_ref, hl_ref, hr_ref, w0_in, g_in, e_in, w1_in, buf_in,
                 out_ref, w0_ref, g_ref, e_ref, w1_ref, s_ref, buf, sems):
    r = Rows(nz)

    def send(source, x):
        return pltpu.make_async_copy(source, out_ref.at[:, :, x, :], sems.at[x])

    inside = [send(buf_in.at[x - 2], x) for x in range(HALO, rows - HALO)]
    for copy in inside:
        copy.start()
    low = iota((8, LANES), 0) < HALO

    def with_halo(local, t, upper):
        at = pl.ds(16 * nz + 8 * t, 8)
        hl, hr = hl_ref[at, :], hr_ref[at, :]
        if upper:
            tile = jnp.where(low, pltpu.roll(hr, HALO, 0), hl)
        else:
            tile = jnp.where(low, hr, pltpu.roll(hl, HALO, 0))
        return jnp.concatenate([local, tile], axis=0)

    strips_of_step(
        strips_of(
            [with_halo(o_ref[k], 2 + k % 2, k >= 2) for k in range(4)],
            [with_halo(l_ref[k], k, False) for k in range(2)],
            [with_halo(r_ref[k], k, True) for k in range(2)],
        ),
        s_ref,
    )
    ring = rows + 2 * HALO

    def x_of(l):
        return l - HALO if l < 10 else l - 16 + rows

    def row(l):
        return lambda n: s_ref[n, pl.ds(x_of(l) % ring, 1), :]

    def either(ref, ref_in, inside):
        def get(n, lt, l):
            if inside <= x_of(l) < rows - inside:
                return ref_in[n, lt, r.at(x_of(l)), :]
            return ref[n, lt, r.at(l), :]

        return get

    def edge(l):
        ref = {3: hl_ref, 4: x_ref.at[0], 15: x_ref.at[1], 16: hr_ref}[l]
        return lambda k, lt, x: ref[r.at(8 + 2 * k + lt), :]

    w0 = either(w0_ref, w0_in, 0)
    for l in (3, 16):
        r.plane(l, [density(edge(l)(0, lt, l)) for lt in range(2)], w0_ref)
    for l, other in ((3, 4), (4, 3), (15, 16), (16, 15)):
        r.first_step(l, g_ref, lambda lt: r.rest(l, other, lt, w0, edge(l)))

    own = either(g_ref, g_in, 1)

    def g(n, lt, l):
        if l == 2 or l == 17:
            ref = hl_ref if l == 2 else hr_ref
            return ref[r.at(2 + 2 * (n % 3) + lt), :]
        return own(n, lt, l)

    for l, ref, n, near in ((2, hl_ref, 6, 3), (17, hr_ref, 3, 16)):
        v = [[ref[r.at(lt), :] + g_ref[n, lt, r.at(near), :]] for lt in range(2)]
        r.plane(l, r.patch(l, v, row(l), e_ref), w1_ref, row(l)(4))
    for l in (3, 4, 5, 14, 15, 16):
        p = r.patch(l, r.gather(l, g), row(l), e_ref)
        r.plane(l, p, w1_ref, row(l)(4))

    for l, x, indices in (
        (6, 2, LEFT),
        (7, 3, STILL + LEFT),
        (12, rows - 4, STILL + RIGHT),
        (13, rows - 3, RIGHT),
    ):
        for i in indices:
            buf[l, i] = buf_in[x - 2, i]

    w1, e = either(w1_ref, w1_in, 2), either(e_ref, e_in, 2)
    edges = []
    for n in (3, 2, 1, 0):
        for l, x in ((n + 3, n), (16 - n, rows - 1 - n)):
            r.second_step(l, w1, e, row(l), buf, 0)
            edges.append(send(buf.at[l + 1 if x == n else l - 1], x))
            edges[-1].start()
    for copy in inside + edges:
        copy.wait()


def body(populations):
    _, nz, rows, columns = populations.shape
    f32 = jnp.float32
    even_x = (lax.axis_index("gx") & 1) == 0
    even_y = (lax.axis_index("gy") & 1) == 0
    vmem = pl.BlockSpec(memory_space=pltpu.VMEM)
    hbm = pl.BlockSpec(memory_space=pltpu.HBM)
    chunks = 4
    params = pltpu.CompilerParams(vmem_limit_bytes=40 * 1024 * 1024)

    def shape(*dims):
        return jax.ShapeDtypeStruct(dims, f32)

    def field(n, count):
        return (n, 2, count * nz, LANES)

    def moments(*refs):
        moments_kernel(nz, chunks, *refs)

    rho, mom, o, to_left, to_right = pl.pallas_call(
        moments,
        out_shape=(
            shape(2, rows * nz, LANES), shape(*field(3, rows)), shape(4, rows, LANES),
            shape(2, rows, LANES), shape(2, rows, LANES),
        ),
        in_specs=[hbm],
        out_specs=(vmem, vmem, vmem, vmem, vmem),
        scratch_shapes=[
            pltpu.VMEM(populations.shape, populations.dtype),
            pltpu.SemaphoreType.DMA((chunks,)),
        ],
        compiler_params=pltpu.CompilerParams(vmem_limit_bytes=50 * 1024 * 1024),
        name="moments",
    )(pltpu.with_memory_space_constraint(populations, pltpu.HBM))

    def both(array_odd, array_even, axis):
        odd = pair_swap(array_odd, axis, 1)
        even = pair_swap(array_even, axis, 0)
        odd = lax.optimization_barrier(-odd)
        return -odd, even

    ob, oa = both(
        jnp.where(even_y, to_left, to_right), jnp.where(even_y, to_right, to_left), "gy"
    )

    left, right = jnp.where(even_y, ob, oa), jnp.where(even_y, oa, ob)

    def early(*refs):
        early_kernel(nz, rows, *refs)

    w0, g, e0, edges = pl.pallas_call(
        early,
        out_shape=(
            shape(*field(4, rows)), shape(*field(9, rows)), shape(*field(4, rows)),
            shape(2, 16 * nz, LANES),
        ),
        in_specs=[vmem, vmem],
        out_specs=(vmem, vmem, vmem, vmem),
        compiler_params=params,
        cost_estimate=pl.CostEstimate(flops=10_000_000, bytes_accessed=2_500_000, transcendentals=0),
        name="early",
    )(rho, mom)

    left, right, edges, e0 = lax.optimization_barrier((left, right, edges, e0))

    def edge(low):
        c = slice(0, HALO) if low else slice(rows - HALO, rows)
        return jnp.concatenate([
            edges[0 if low else 1],
            jnp.concatenate([left[:, c], right[:, c]], axis=1).reshape(-1, LANES),
            jnp.concatenate([o[:2, c], o[2:, c]], axis=1).reshape(-1, LANES),
        ])

    low, high = edge(True), edge(False)
    hb, ha = both(jnp.where(even_x, low, high), jnp.where(even_x, high, low), "gx")

    def inner(*refs):
        inner_kernel(nz, rows, *refs)

    buf, e, w1 = pl.pallas_call(
        inner,
        out_shape=(
            shape(rows - HALO, 19, nz, columns), shape(*field(4, rows)), shape(*field(4, rows)),
        ),
        in_specs=[vmem] * 4,
        out_specs=(vmem, vmem, vmem),
        scratch_shapes=[pltpu.VMEM((10, rows, LANES), f32)],
        compiler_params=params,
        cost_estimate=pl.CostEstimate(flops=10_000_000, bytes_accessed=2_500_000, transcendentals=0),
        name="inner",
    )(e0, o, left, right)
    hl, hr = jnp.where(even_x, hb, ha), jnp.where(even_x, ha, hb)

    def outer(*refs):
        outer_kernel(nz, rows, *refs)

    ring = rows + 2 * HALO
    return pl.pallas_call(
        outer,
        out_shape=shape(*populations.shape),
        in_specs=[vmem] * 11,
        out_specs=hbm,
        scratch_shapes=[
            pltpu.VMEM(field(4, 20), f32),
            pltpu.VMEM(field(9, 20), f32),
            pltpu.VMEM(field(4, 20), f32),
            pltpu.VMEM(field(4, 20), f32),
            pltpu.VMEM((10, ring, LANES), f32),
            pltpu.VMEM((20, 19, nz, columns), f32),
            pltpu.SemaphoreType.DMA((rows,)),
        ],
        compiler_params=params,
        name="outer",
    )(edges, o, left, right, hl, hr, w0, g, e, w1, buf)


def solution(mesh):
    return jax.shard_map(
        body,
        mesh=mesh,
        in_specs=(P(None, None, "gx", "gy"),),
        out_specs=P(None, None, "gx", "gy"),
        check_vma=False,
    )
```

```python
import jax
import jax.numpy as jnp
from jax import lax
from jax.experimental import pallas as pl
from jax.experimental.pallas import tpu as pltpu
from jax.sharding import PartitionSpec as P

HALO = 4
LANES = 128
STILL = (0, 3, 4, 5, 6, 15, 16, 17, 18)
RIGHT = (1, 7, 9, 11, 13)
LEFT = (2, 8, 10, 12, 14)


def pair_swap(array, axis, odd):
    size = lax.axis_size(axis)
    pairs = []
    for low in range(odd, size + odd, 2):
        a, b = low % size, (low + 1) % size
        pairs += [(a, b), (b, a)]
    return lax.ppermute(array, axis, pairs)


def iota(shape, dim):
    return lax.broadcasted_iota(jnp.int32, shape, dim)


def density(v):
    return 1.0 - jnp.exp(-v)


def loop(lo, hi, fn, unroll=4):
    count = (hi - lo) // unroll

    def group(i, c):
        for j in range(unroll):
            fn(lo + i * unroll + j)
        return c

    lax.fori_loop(0, count, group, 0)
    for left in range(lo + count * unroll, hi, 2):
        step = min(2, hi - left)
        lax.fori_loop(left, left + 1, lambda i, c: ([fn(i + j) for j in range(step)], c)[1], 0)


def moments_kernel(nz, chunks, pop_ref, rho_ref, mom_ref, o_ref, l_ref, r_ref, buf, sems):
    step = nz // chunks
    copies = []
    for c in range(chunks):
        part = pl.ds(c * step, step)
        copies.append(pltpu.make_async_copy(pop_ref.at[:, part], buf.at[:, part], sems.at[c]))
        copies[-1].start()
    rows = buf.shape[2]
    lane = iota((rows, LANES), 1)

    def plane(z, packed):
        tiles = []
        for lt in range(2):
            cols = slice(lt * LANES, (lt + 1) * LANES)

            def f(i):
                return buf[i, z, :, cols].astype(jnp.float32)

            rho, jx, jy, jz = f(0), None, None, None
            f1, f2 = f(1), f(2)
            rho, jx = rho + (f1 + f2), f1 - f2
            f1, f2 = f(3), f(4)
            rho, jy = rho + (f1 + f2), f1 - f2
            f1, f2 = f(5), f(6)
            rho, jz = rho + (f1 + f2), f1 - f2
            f1, f2 = f(7), f(8)
            d = f1 - f2
            rho, jx, jy = rho + (f1 + f2), jx + d, jy + d
            f1, f2 = f(9), f(10)
            d = f1 - f2
            rho, jx, jy = rho + (f1 + f2), jx + d, jy - d
            f1, f2 = f(11), f(12)
            d = f1 - f2
            rho, jx, jz = rho + (f1 + f2), jx + d, jz + d
            f1, f2 = f(13), f(14)
            d = f1 - f2
            rho, jx, jz = rho + (f1 + f2), jx + d, jz - d
            f1, f2 = f(15), f(16)
            d = f1 - f2
            rho, jy, jz = rho + (f1 + f2), jy + d, jz + d
            f1, f2 = f(17), f(18)
            d = f1 - f2
            rho, jy, jz = rho + (f1 + f2), jy + d, jz - d
            tiles.append((rho, jx, jy, jz))
        out = []
        group = nz - 1 - z
        shift = lax.rem(group * 8 + 4, LANES)
        for k in range(4):
            both = jnp.where(lane >= LANES - HALO, tiles[1][k], tiles[0][k])
            out.append(jnp.where(lane // 8 == group, pltpu.roll(both, shift, 1), packed[k]))
            for lt in range(2):
                v = tiles[lt][k]
                for x in range(0, rows, 8):
                    at = pl.ds(x * nz + z, 8, stride=nz)
                    if k == 0:
                        rho_ref[lt, at, :] = v[x : x + 8]
                    else:
                        mom_ref[k - 1, lt, at, :] = v[x : x + 8]
        return tuple(out)

    packed = (jnp.zeros((rows, LANES), jnp.float32),) * 4
    for c in range(chunks):
        copies[c].wait()

        def group(i, t, c=c):
            for j in range(4):
                t = plane(c * step + 4 * i + j, t)
            return t

        packed = lax.fori_loop(0, step // 4, group, packed)
    for k in range(4):
        o_ref[k] = packed[k]
    high = (lane & 7) < HALO
    for n in range(2):
        a, b = packed[2 * n : 2 * n + 2]
        l_ref[n] = jnp.where(high, pltpu.roll(b, LANES - HALO, 1), a)
        r_ref[n] = jnp.where(high, a, pltpu.roll(b, HALO, 1))


def strips_of(o, left, right):
    own = (iota(o[0].shape, 1) & 7) < HALO
    ls, rs = [], []
    for n in range(2):
        a, b = o[2 * n : 2 * n + 2]
        ls += [jnp.where(own, left[n], a), jnp.where(own, pltpu.roll(left[n], LANES - HALO, 1), b)]
        rs += [jnp.where(own, a, right[n]), jnp.where(own, b, pltpu.roll(right[n], HALO, 1))]
    return ls, rs


def pushed(p, force, momentum):
    scale = p * (1.0 / 6.0)
    return [j + scale * f for j, f in zip(momentum, force)]


def post_of(rho, momentum):
    inv = 1.0 / rho
    ux, uy, uz = [j * inv for j in momentum]
    r36 = rho * (1.0 / 36.0)
    r3 = rho * (1.0 / 12.0)
    ox, oy, oz = r3 * ux, r3 * uy, r3 * uz
    hx, hy, hz = 1.5 * ux, 1.5 * uy, 1.5 * uz
    xx, yy, zz = hx * ox, hy * oy, hz * oz
    k = r36 - (xx + yy + zz) * (1.0 / 3.0)
    kx, ky, kz = k + xx, k + yy, k + zz
    out = [12.0 * k]
    for e, o in ((kx, ox), (ky, oy), (kz, oz)):
        e2, o2 = e + e, o + o
        out += [e2 + o2, e2 - o2]
    for e, a, b, h in ((kx + yy, ox, oy, hx), (kx + zz, ox, oz, hx), (ky + zz, oy, oz, hy)):
        cross = h * b
        cross = cross + cross
        ep, em = e + cross, e - cross
        op, om = a + b, a - b
        out += [ep + op, ep - op, em + om, em - om]
    return out


def strips_of_step(strips, s_ref):
    def xp(a):
        return pltpu.roll(a, a.shape[0] - 1, 0)

    def xm(a):
        return pltpu.roll(a, 1, 0)

    def ym(a):
        return pltpu.roll(a, 1, 1)

    def yp(a):
        return pltpu.roll(a, LANES - 1, 1)

    def zm(a):
        return pltpu.roll(a, LANES - 8, 1)

    def zp(a):
        return pltpu.roll(a, 8, 1)

    def post(p, v):
        a, b = ym(p), yp(p)
        q, d = p + p + (a + b), b - a
        bb = q + (xp(p) + xm(p))
        aa = q + (zp(p) + zm(p))
        fx = xp(aa) - xm(aa)
        fy = d + d + (xp(d) + xm(d)) + (zp(d) + zm(d))
        fz = zp(bb) - zm(bb)
        return post_of(v[0], pushed(p, (fx, fy, fz), v[1:]))

    own = (iota(strips[0][0].shape, 1) & 7) < HALO
    moments, later = [], []
    for side, v in enumerate(strips):
        f = post(density(v[0]), v)
        a15, a17, a18, a16 = zm(f[15]), zp(f[17]), zm(f[18]), zp(f[16])
        sp, jp = ym(f[3] + (a15 + a17)), ym(a15 - a17)
        sn, jn = yp(f[4] + (a18 + a16)), yp(a18 - a16)
        a, b = zm(f[5]), zp(f[6])
        r0, jz0, jy0 = f[0] + (a + b) + (sp + sn), (a - b) + (jp + jn), sp - sn
        a, b, c, e = ym(f[7]), yp(f[9]), zm(f[11]), zp(f[13])
        ru, jyu, jzu = xm(f[1] + (a + b) + (c + e)), xm(a - b), xm(c - e)
        a, b, c, e = ym(f[10]), yp(f[8]), zm(f[14]), zp(f[12])
        rd, jyd, jzd = xp(f[2] + (a + b) + (c + e)), xp(a - b), xp(c - e)
        v = (r0 + (ru + rd), ru - rd, jy0 + (jyu + jyd), jz0 + (jzu + jzd))
        moments.append(v)
        p = density(v[0])
        f = post(p, v)
        if side == 0:
            later.append((p, f[3], zm(f[15]), zp(f[17]), f[7], f[10]))
        else:
            later.append((p, f[4], zp(f[16]), zm(f[18]), f[8], f[9]))
    for k in range(4):
        s_ref[k] = jnp.where(own, moments[1][k], moments[0][k])
    lane = iota(own.shape, 1) & 7
    for n in range(6):
        s_ref[4 + n] = jnp.where(lane == HALO - 1, later[0][n], pltpu.roll(later[1][n], LANES - 2, 1))


class Rows:
    def __init__(self, nz):
        self.nz = nz
        lane = iota((nz, LANES), 1)
        self.first, self.last = lane == 0, lane == LANES - 1
        self.two = lane < 2, lane >= LANES - 2

    def at(self, x):
        if isinstance(x, int):
            return pl.ds(x * self.nz, self.nz)
        return pl.ds(pl.multiple_of(x * self.nz, self.nz), self.nz)

    def of(self, ref):
        return lambda n, lt, x: ref[n, lt, self.at(x), :]

    def zp(self, v):
        return pltpu.roll(v, self.nz - 1, 0)

    def zm(self, v):
        return pltpu.roll(v, 1, 0)

    def edge(self, row, shift):
        wide = jnp.broadcast_to(row, (8, LANES))
        return jnp.concatenate(
            [pltpu.roll(wide, shift + 8 * z, 1, stride=8, stride_axis=0) for z in range(0, self.nz, 8)],
            axis=0,
        )

    def ym(self, a, h=None):
        r0, r1 = pltpu.roll(a[0], 1, 1), pltpu.roll(a[1], 1, 1)
        return r0 if h is None else jnp.where(self.first, h, r0), jnp.where(self.first, r0, r1)

    def yp(self, a, h=None):
        r0, r1 = pltpu.roll(a[0], LANES - 1, 1), pltpu.roll(a[1], LANES - 1, 1)
        return jnp.where(self.last, r1, r0), r1 if h is None else jnp.where(self.last, h, r1)

    def plane(self, x, p, w_ref, row=None):
        h = None if row is None else self.edge(row, 5)
        a, b = self.ym(p, h), self.yp(p, h)
        for lt in range(2):
            q = p[lt] + p[lt] + (a[lt] + b[lt])
            w_ref[0, lt, self.at(x), :] = p[lt]
            w_ref[1, lt, self.at(x), :] = q
            w_ref[2, lt, self.at(x), :] = q + (self.zp(p[lt]) + self.zm(p[lt]))
            w_ref[3, lt, self.at(x), :] = b[lt] - a[lt]

    def posts(self, x, lt, w, v):
        bb = w(1, lt, x) + (w(0, lt, x + 1) + w(0, lt, x - 1))
        dd = w(3, lt, x)
        fx = w(2, lt, x + 1) - w(2, lt, x - 1)
        fy = dd + dd + (self.zp(dd) + self.zm(dd)) + (w(3, lt, x + 1) + w(3, lt, x - 1))
        fz = self.zp(bb) - self.zm(bb)
        m = pushed(w(0, lt, x), (fx, fy, fz), [v(k, lt, x) for k in (1, 2, 3)])
        return post_of(v(0, lt, x), m)

    def half(self, x, other, lt, w, v):
        bb = w(1, lt, x) + w(0, lt, other)
        dd = w(3, lt, x)
        fx = w(2, lt, other) if other > x else -w(2, lt, other)
        fy = dd + dd + (self.zp(dd) + self.zm(dd)) + w(3, lt, other)
        fz = self.zp(bb) - self.zm(bb)
        return pushed(w(0, lt, x), (fx, fy, fz), [v(k, lt, x) for k in (1, 2, 3)])

    def rest(self, x, other, lt, w, v):
        p = w(0, lt, other)
        fx = w(2, lt, other) if other > x else -w(2, lt, other)
        fz = self.zp(p) - self.zm(p)
        m = pushed(w(0, lt, x), (fx, w(3, lt, other), fz), [v(k, lt, x) for k in (1, 2, 3)])
        return post_of(v(0, lt, x), m)

    def first_step(self, x, g_ref, posts):
        zp, zm = self.zp, self.zm
        part, left, right = [], [], []
        for lt in range(2):
            f = posts(lt)
            a15, a17, a18, a16 = zm(f[15]), zp(f[17]), zm(f[18]), zp(f[16])
            left.append((f[3] + (a15 + a17), a15 - a17, f[7], f[10]))
            right.append((f[4] + (a18 + a16), a18 - a16, f[9], f[8]))
            a, b = zm(f[5]), zp(f[6])
            s = [f[0] + (a + b), a - b]
            a, b = zm(f[11]), zp(f[13])
            s += [f[1] + (a + b), a - b]
            a, b = zm(f[14]), zp(f[12])
            s += [f[2] + (a + b), a - b]
            part.append(s)
        m = [self.ym((left[0][n], left[1][n])) for n in range(4)]
        q = [self.yp((right[0][n], right[1][n])) for n in range(4)]
        for lt in range(2):
            s = part[lt]

            def put(n, value):
                g_ref[n, lt, self.at(x), :] = value

            put(0, s[0] + (m[0][lt] + q[0][lt]))
            put(1, m[0][lt] - q[0][lt])
            put(2, s[1] + (m[1][lt] + q[1][lt]))
            put(3, s[2] + (m[2][lt] + q[2][lt]))
            put(4, m[2][lt] - q[2][lt])
            put(5, s[3])
            put(6, s[4] + (m[3][lt] + q[3][lt]))
            put(7, m[3][lt] - q[3][lt])
            put(8, s[5])

    def gather(self, x, g):
        out = []
        for lt in range(2):
            ru, rd = g(3, lt, x - 1), g(6, lt, x + 1)
            v = [g(0, lt, x) + (ru + rd), ru - rd]
            for k in (1, 2):
                v.append(g(k, lt, x) + (g(k + 3, lt, x - 1) + g(k + 6, lt, x + 1)))
            out.append(v)
        return out

    def patch(self, x, v, row, e_ref):
        for k in range(len(v[0])):
            h = self.edge(row(k), 4)
            v[0][k] = jnp.where(self.two[0], h, v[0][k])
            v[1][k] = jnp.where(self.two[1], h, v[1][k])
            for lt in range(2):
                e_ref[k, lt, self.at(x), :] = v[lt][k]
        return [density(v[0][0]), density(v[1][0])]

    def second_step(self, x, w, e, row, buf, shift):
        zp, zm = self.zp, self.zm
        left, right = [], []
        n, u, d = x + shift, x + shift + 1, x + shift - 1

        def put(i, row, lt, v):
            buf[row, i, :, lt * LANES : (lt + 1) * LANES] = v

        for lt in range(2):
            f = self.posts(x, lt, w, e)
            put(0, n, lt, f[0])
            put(5, n, lt, zm(f[5]))
            put(6, n, lt, zp(f[6]))
            put(1, u, lt, f[1])
            put(11, u, lt, zm(f[11]))
            put(13, u, lt, zp(f[13]))
            put(2, d, lt, f[2])
            put(12, d, lt, zp(f[12]))
            put(14, d, lt, zm(f[14]))
            left.append((f[3], zm(f[15]), zp(f[17]), f[7], f[10]))
            right.append((f[4], zp(f[16]), zm(f[18]), f[8], f[9]))
        h = [self.edge(row(5 + j), 5) for j in range(5)]
        for j, (i, to) in enumerate(((3, n), (15, n), (17, n), (7, u), (10, d))):
            v = self.ym((left[0][j], left[1][j]), h[j])
            put(i, to, 0, v[0])
            put(i, to, 1, v[1])
        for j, (i, to) in enumerate(((4, n), (16, n), (18, n), (8, d), (9, u))):
            v = self.yp((right[0][j], right[1][j]), h[j])
            put(i, to, 0, v[0])
            put(i, to, 1, v[1])


def early_kernel(nz, rows, rho_ref, mom_ref, w_ref, g_ref, e_ref, x_ref):
    r = Rows(nz)
    w, g = r.of(w_ref), r.of(g_ref)

    def v(k, lt, x):
        return rho_ref[lt, r.at(x), :] if k == 0 else mom_ref[k - 1, lt, r.at(x), :]

    def start(x):
        r.plane(x, [density(rho_ref[lt, r.at(x), :]) for lt in range(2)], w_ref)

    def first(x):
        r.first_step(x, g_ref, lambda lt: r.posts(x, lt, w, v))

    def middle(x):
        v = r.gather(x, g)
        for lt in range(2):
            for k in range(4):
                e_ref[k, lt, r.at(x), :] = v[lt][k]

    loop(0, rows, start, 16)
    for side, x, other in ((0, 0, 1), (1, rows - 1, rows - 2)):
        for lt in range(2):
            x_ref[side, r.at(8 + lt), :] = v(0, lt, x)
            for k, j in enumerate(r.half(x, other, lt, w, v)):
                x_ref[side, r.at(10 + 2 * k + lt), :] = j
    loop(1, rows - 1, first, 14)
    loop(2, rows - 2, middle, 12)
    for side, base, x, other in ((0, 6, 1, 2), (1, 3, rows - 2, rows - 3)):
        for lt in range(2):
            x_ref[side, r.at(lt), :] = g(0, lt, x) + g(base, lt, other)
            for k in range(3):
                x_ref[side, r.at(2 + 2 * k + lt), :] = g(base + k, lt, x)


def inner_kernel(nz, rows, e_in, o_ref, l_ref, r_ref, buf, e_ref, w_ref, s_ref):
    r = Rows(nz)
    strips_of_step(
        strips_of(
            [o_ref[k] for k in range(4)], [l_ref[k] for k in range(2)], [r_ref[k] for k in range(2)]
        ),
        s_ref,
    )

    def row(x):
        return lambda n: s_ref[n, pl.ds(x, 1), :]

    def middle(x):
        v = [[e_in[k, lt, r.at(x), :] for k in range(4)] for lt in range(2)]
        p = r.patch(x, v, row(x), e_ref)
        r.plane(x, p, w_ref, row(x)(4))

    def second(x):
        r.second_step(x, r.of(w_ref), r.of(e_ref), row(x), buf, -2)

    loop(2, rows - 2, middle, 12)
    loop(3, rows - 3, second, 10)


def outer_kernel(nz, rows, x_ref, o_ref, l_ref, r_ref, hl_ref, hr_ref, w0_in, g_in, e_in, w1_in, buf_in,
                 out_ref, w0_ref, g_ref, e_ref, w1_ref, s_ref, buf, sems):
    r = Rows(nz)

    def send(source, x):
        return pltpu.make_async_copy(source, out_ref.at[:, :, x, :], sems.at[x])

    inside = [send(buf_in.at[x - 2], x) for x in range(HALO, rows - HALO)]
    for copy in inside[:2]:
        copy.start()
    low = iota((8, LANES), 0) < HALO

    def with_halo(local, t, upper):
        at = pl.ds(16 * nz + 8 * t, 8)
        hl, hr = hl_ref[at, :], hr_ref[at, :]
        if upper:
            tile = jnp.where(low, pltpu.roll(hr, HALO, 0), hl)
        else:
            tile = jnp.where(low, hr, pltpu.roll(hl, HALO, 0))
        return jnp.concatenate([local, tile], axis=0)

    strips_of_step(
        strips_of(
            [with_halo(o_ref[k], 2 + k % 2, k >= 2) for k in range(4)],
            [with_halo(l_ref[k], k, False) for k in range(2)],
            [with_halo(r_ref[k], k, True) for k in range(2)],
        ),
        s_ref,
    )
    ring = rows + 2 * HALO

    def x_of(l):
        return l - HALO if l < 10 else l - 16 + rows

    def row(l):
        return lambda n: s_ref[n, pl.ds(x_of(l) % ring, 1), :]

    def either(ref, ref_in, inside):
        def get(n, lt, l):
            if inside <= x_of(l) < rows - inside:
                return ref_in[n, lt, r.at(x_of(l)), :]
            return ref[n, lt, r.at(l), :]

        return get

    def edge(l):
        ref = {3: hl_ref, 4: x_ref.at[0], 15: x_ref.at[1], 16: hr_ref}[l]
        return lambda k, lt, x: ref[r.at(8 + 2 * k + lt), :]

    w0 = either(w0_ref, w0_in, 0)
    for l in (3, 16):
        r.plane(l, [density(edge(l)(0, lt, l)) for lt in range(2)], w0_ref)
    for l, other in ((3, 4), (4, 3), (15, 16), (16, 15)):
        r.first_step(l, g_ref, lambda lt: r.rest(l, other, lt, w0, edge(l)))

    for copy in inside[2:]:
        copy.start()
    own = either(g_ref, g_in, 1)

    def g(n, lt, l):
        if l == 2 or l == 17:
            ref = hl_ref if l == 2 else hr_ref
            return ref[r.at(2 + 2 * (n % 3) + lt), :]
        return own(n, lt, l)

    for l, ref, n, near in ((2, hl_ref, 6, 3), (17, hr_ref, 3, 16)):
        v = [[ref[r.at(lt), :] + g_ref[n, lt, r.at(near), :]] for lt in range(2)]
        r.plane(l, r.patch(l, v, row(l), e_ref), w1_ref, row(l)(4))
    for l in (3, 4, 5, 14, 15, 16):
        p = r.patch(l, r.gather(l, g), row(l), e_ref)
        r.plane(l, p, w1_ref, row(l)(4))

    for l, x, indices in (
        (6, 2, LEFT),
        (7, 3, STILL + LEFT),
        (12, rows - 4, STILL + RIGHT),
        (13, rows - 3, RIGHT),
    ):
        for i in indices:
            buf[l, i] = buf_in[x - 2, i]

    w1, e = either(w1_ref, w1_in, 2), either(e_ref, e_in, 2)
    edges = []
    for side in range(2):
        for n in (3, 2, 1, 0):
            l, x = ((n + 3, n), (16 - n, rows - 1 - n))[side]
            r.second_step(l, w1, e, row(l), buf, 0)
            edges.append(send(buf.at[l + 1 if x == n else l - 1], x))
            edges[-1].start()
    for copy in inside + edges:
        copy.wait()


def body(populations):
    _, nz, rows, columns = populations.shape
    f32 = jnp.float32
    even_x = (lax.axis_index("gx") & 1) == 0
    even_y = (lax.axis_index("gy") & 1) == 0
    vmem = pl.BlockSpec(memory_space=pltpu.VMEM)
    hbm = pl.BlockSpec(memory_space=pltpu.HBM)
    chunks = 4
    params = pltpu.CompilerParams(vmem_limit_bytes=40 * 1024 * 1024)

    def shape(*dims):
        return jax.ShapeDtypeStruct(dims, f32)

    def field(n, count):
        return (n, 2, count * nz, LANES)

    def moments(*refs):
        moments_kernel(nz, chunks, *refs)

    rho, mom, o, to_left, to_right = pl.pallas_call(
        moments,
        out_shape=(
            shape(2, rows * nz, LANES), shape(*field(3, rows)), shape(4, rows, LANES),
            shape(2, rows, LANES), shape(2, rows, LANES),
        ),
        in_specs=[hbm],
        out_specs=(vmem, vmem, vmem, vmem, vmem),
        scratch_shapes=[
            pltpu.VMEM(populations.shape, populations.dtype),
            pltpu.SemaphoreType.DMA((chunks,)),
        ],
        compiler_params=pltpu.CompilerParams(vmem_limit_bytes=50 * 1024 * 1024),
        name="moments",
    )(pltpu.with_memory_space_constraint(populations, pltpu.HBM))

    def both(array_odd, array_even, axis):
        odd = pair_swap(array_odd, axis, 1)
        even = pair_swap(array_even, axis, 0)
        odd = lax.optimization_barrier(-odd)
        return -odd, even

    ob, oa = both(
        jnp.where(even_y, to_left, to_right), jnp.where(even_y, to_right, to_left), "gy"
    )

    left, right = jnp.where(even_y, ob, oa), jnp.where(even_y, oa, ob)

    def early(*refs):
        early_kernel(nz, rows, *refs)

    w0, g, e0, edges = pl.pallas_call(
        early,
        out_shape=(
            shape(*field(4, rows)), shape(*field(9, rows)), shape(*field(4, rows)),
            shape(2, 16 * nz, LANES),
        ),
        in_specs=[vmem, vmem],
        out_specs=(vmem, vmem, vmem, vmem),
        compiler_params=params,
        cost_estimate=pl.CostEstimate(flops=10_000_000, bytes_accessed=2_500_000, transcendentals=0),
        name="early",
    )(rho, mom)

    left, right, edges, e0 = lax.optimization_barrier((left, right, edges, e0))

    def edge(low):
        c = slice(0, HALO) if low else slice(rows - HALO, rows)
        return jnp.concatenate([
            edges[0 if low else 1],
            jnp.concatenate([left[:, c], right[:, c]], axis=1).reshape(-1, LANES),
            jnp.concatenate([o[:2, c], o[2:, c]], axis=1).reshape(-1, LANES),
        ])

    low, high = edge(True), edge(False)
    hb, ha = both(jnp.where(even_x, low, high), jnp.where(even_x, high, low), "gx")

    def inner(*refs):
        inner_kernel(nz, rows, *refs)

    buf, e, w1 = pl.pallas_call(
        inner,
        out_shape=(
            shape(rows - HALO, 19, nz, columns), shape(*field(4, rows)), shape(*field(4, rows)),
        ),
        in_specs=[vmem] * 4,
        out_specs=(vmem, vmem, vmem),
        scratch_shapes=[pltpu.VMEM((10, rows, LANES), f32)],
        compiler_params=params,
        cost_estimate=pl.CostEstimate(flops=10_000_000, bytes_accessed=2_500_000, transcendentals=0),
        name="inner",
    )(e0, o, left, right)
    hl, hr = jnp.where(even_x, hb, ha), jnp.where(even_x, ha, hb)

    def outer(*refs):
        outer_kernel(nz, rows, *refs)

    ring = rows + 2 * HALO
    return pl.pallas_call(
        outer,
        out_shape=shape(*populations.shape),
        in_specs=[vmem] * 11,
        out_specs=hbm,
        scratch_shapes=[
            pltpu.VMEM(field(4, 20), f32),
            pltpu.VMEM(field(9, 20), f32),
            pltpu.VMEM(field(4, 20), f32),
            pltpu.VMEM(field(4, 20), f32),
            pltpu.VMEM((10, ring, LANES), f32),
            pltpu.VMEM((20, 19, nz, columns), f32),
            pltpu.SemaphoreType.DMA((rows,)),
        ],
        compiler_params=params,
        name="outer",
    )(edges, o, left, right, hl, hr, w0, g, e, w1, buf)


def solution(mesh):
    return jax.shard_map(
        body,
        mesh=mesh,
        in_specs=(P(None, None, "gx", "gy"),),
        out_specs=P(None, None, "gx", "gy"),
        check_vma=False,
    )
```

```python
import jax
import jax.numpy as jnp
from jax import lax
from jax.experimental import pallas as pl
from jax.experimental.pallas import tpu as pltpu
from jax.sharding import PartitionSpec as P

HALO = 4
LANES = 128
STILL = (0, 3, 4, 5, 6, 15, 16, 17, 18)
RIGHT = (1, 7, 9, 11, 13)
LEFT = (2, 8, 10, 12, 14)


def pair_swap(array, axis, odd):
    size = lax.axis_size(axis)
    pairs = []
    for low in range(odd, size + odd, 2):
        a, b = low % size, (low + 1) % size
        pairs += [(a, b), (b, a)]
    return lax.ppermute(array, axis, pairs)


def iota(shape, dim):
    return lax.broadcasted_iota(jnp.int32, shape, dim)


def density(v):
    return 1.0 - jnp.exp(-v)


def loop(lo, hi, fn, unroll=4):
    count = (hi - lo) // unroll

    def group(i, c):
        for j in range(unroll):
            fn(lo + i * unroll + j)
        return c

    lax.fori_loop(0, count, group, 0)
    for left in range(lo + count * unroll, hi, 2):
        step = min(2, hi - left)
        lax.fori_loop(left, left + 1, lambda i, c: ([fn(i + j) for j in range(step)], c)[1], 0)


def moments_kernel(nz, chunks, pop_ref, rho_ref, mom_ref, o_ref, l_ref, r_ref, buf, sems):
    step = nz // chunks
    copies = []
    for c in range(chunks):
        part = pl.ds(c * step, step)
        copies.append(pltpu.make_async_copy(pop_ref.at[:, part], buf.at[:, part], sems.at[c]))
        copies[-1].start()
    rows = buf.shape[2]
    lane = iota((rows, LANES), 1)

    def plane(z, packed):
        tiles = []
        for lt in range(2):
            cols = slice(lt * LANES, (lt + 1) * LANES)

            def f(i):
                return buf[i, z, :, cols].astype(jnp.float32)

            rho, jx, jy, jz = f(0), None, None, None
            f1, f2 = f(1), f(2)
            rho, jx = rho + (f1 + f2), f1 - f2
            f1, f2 = f(3), f(4)
            rho, jy = rho + (f1 + f2), f1 - f2
            f1, f2 = f(5), f(6)
            rho, jz = rho + (f1 + f2), f1 - f2
            f1, f2 = f(7), f(8)
            d = f1 - f2
            rho, jx, jy = rho + (f1 + f2), jx + d, jy + d
            f1, f2 = f(9), f(10)
            d = f1 - f2
            rho, jx, jy = rho + (f1 + f2), jx + d, jy - d
            f1, f2 = f(11), f(12)
            d = f1 - f2
            rho, jx, jz = rho + (f1 + f2), jx + d, jz + d
            f1, f2 = f(13), f(14)
            d = f1 - f2
            rho, jx, jz = rho + (f1 + f2), jx + d, jz - d
            f1, f2 = f(15), f(16)
            d = f1 - f2
            rho, jy, jz = rho + (f1 + f2), jy + d, jz + d
            f1, f2 = f(17), f(18)
            d = f1 - f2
            rho, jy, jz = rho + (f1 + f2), jy + d, jz - d
            tiles.append((rho, jx, jy, jz))
        out = []
        group = nz - 1 - z
        shift = lax.rem(group * 8 + 4, LANES)
        for k in range(4):
            both = jnp.where(lane >= LANES - HALO, tiles[1][k], tiles[0][k])
            out.append(jnp.where(lane // 8 == group, pltpu.roll(both, shift, 1), packed[k]))
            for lt in range(2):
                v = tiles[lt][k]
                for x in range(0, rows, 8):
                    at = pl.ds(x * nz + z, 8, stride=nz)
                    if k == 0:
                        rho_ref[lt, at, :] = v[x : x + 8]
                    else:
                        mom_ref[k - 1, lt, at, :] = v[x : x + 8]
        return tuple(out)

    packed = (jnp.zeros((rows, LANES), jnp.float32),) * 4
    for c in range(chunks):
        copies[c].wait()

        def group(i, t, c=c):
            for j in range(4):
                t = plane(c * step + 4 * i + j, t)
            return t

        packed = lax.fori_loop(0, step // 4, group, packed)
    for k in range(4):
        o_ref[k] = packed[k]
    high = (lane & 7) < HALO
    for n in range(2):
        a, b = packed[2 * n : 2 * n + 2]
        l_ref[n] = jnp.where(high, pltpu.roll(b, LANES - HALO, 1), a)
        r_ref[n] = jnp.where(high, a, pltpu.roll(b, HALO, 1))


def strips_of(o, left, right):
    own = (iota(o[0].shape, 1) & 7) < HALO
    ls, rs = [], []
    for n in range(2):
        a, b = o[2 * n : 2 * n + 2]
        ls += [jnp.where(own, left[n], a), jnp.where(own, pltpu.roll(left[n], LANES - HALO, 1), b)]
        rs += [jnp.where(own, a, right[n]), jnp.where(own, b, pltpu.roll(right[n], HALO, 1))]
    return ls, rs


def pushed(p, force, momentum):
    scale = p * (1.0 / 6.0)
    return [j + scale * f for j, f in zip(momentum, force)]


def post_of(rho, momentum):
    inv = 1.0 / rho
    ux, uy, uz = [j * inv for j in momentum]
    r36 = rho * (1.0 / 36.0)
    r3 = rho * (1.0 / 12.0)
    ox, oy, oz = r3 * ux, r3 * uy, r3 * uz
    hx, hy, hz = 1.5 * ux, 1.5 * uy, 1.5 * uz
    xx, yy, zz = hx * ox, hy * oy, hz * oz
    k = r36 - (xx + yy + zz) * (1.0 / 3.0)
    kx, ky, kz = k + xx, k + yy, k + zz
    out = [12.0 * k]
    for e, o in ((kx, ox), (ky, oy), (kz, oz)):
        e2, o2 = e + e, o + o
        out += [e2 + o2, e2 - o2]
    for e, a, b, h in ((kx + yy, ox, oy, hx), (kx + zz, ox, oz, hx), (ky + zz, oy, oz, hy)):
        cross = h * b
        cross = cross + cross
        ep, em = e + cross, e - cross
        op, om = a + b, a - b
        out += [ep + op, ep - op, em + om, em - om]
    return out


def strips_of_step(strips, s_ref):
    def xp(a):
        return pltpu.roll(a, a.shape[0] - 1, 0)

    def xm(a):
        return pltpu.roll(a, 1, 0)

    def ym(a):
        return pltpu.roll(a, 1, 1)

    def yp(a):
        return pltpu.roll(a, LANES - 1, 1)

    def zm(a):
        return pltpu.roll(a, LANES - 8, 1)

    def zp(a):
        return pltpu.roll(a, 8, 1)

    def post(p, v):
        a, b = ym(p), yp(p)
        q, d = p + p + (a + b), b - a
        bb = q + (xp(p) + xm(p))
        aa = q + (zp(p) + zm(p))
        fx = xp(aa) - xm(aa)
        fy = d + d + (xp(d) + xm(d)) + (zp(d) + zm(d))
        fz = zp(bb) - zm(bb)
        return post_of(v[0], pushed(p, (fx, fy, fz), v[1:]))

    own = (iota(strips[0][0].shape, 1) & 7) < HALO
    moments, later = [], []
    for side, v in enumerate(strips):
        f = post(density(v[0]), v)
        a15, a17, a18, a16 = zm(f[15]), zp(f[17]), zm(f[18]), zp(f[16])
        sp, jp = ym(f[3] + (a15 + a17)), ym(a15 - a17)
        sn, jn = yp(f[4] + (a18 + a16)), yp(a18 - a16)
        a, b = zm(f[5]), zp(f[6])
        r0, jz0, jy0 = f[0] + (a + b) + (sp + sn), (a - b) + (jp + jn), sp - sn
        a, b, c, e = ym(f[7]), yp(f[9]), zm(f[11]), zp(f[13])
        ru, jyu, jzu = xm(f[1] + (a + b) + (c + e)), xm(a - b), xm(c - e)
        a, b, c, e = ym(f[10]), yp(f[8]), zm(f[14]), zp(f[12])
        rd, jyd, jzd = xp(f[2] + (a + b) + (c + e)), xp(a - b), xp(c - e)
        v = (r0 + (ru + rd), ru - rd, jy0 + (jyu + jyd), jz0 + (jzu + jzd))
        moments.append(v)
        p = density(v[0])
        f = post(p, v)
        if side == 0:
            later.append((p, f[3], zm(f[15]), zp(f[17]), f[7], f[10]))
        else:
            later.append((p, f[4], zp(f[16]), zm(f[18]), f[8], f[9]))
    for k in range(4):
        s_ref[k] = jnp.where(own, moments[1][k], moments[0][k])
    lane = iota(own.shape, 1) & 7
    for n in range(6):
        s_ref[4 + n] = jnp.where(lane == HALO - 1, later[0][n], pltpu.roll(later[1][n], LANES - 2, 1))


class Rows:
    def __init__(self, nz):
        self.nz = nz
        lane = iota((nz, LANES), 1)
        self.first, self.last = lane == 0, lane == LANES - 1
        self.two = lane < 2, lane >= LANES - 2

    def at(self, x):
        if isinstance(x, int):
            return pl.ds(x * self.nz, self.nz)
        return pl.ds(pl.multiple_of(x * self.nz, self.nz), self.nz)

    def of(self, ref):
        return lambda n, lt, x: ref[n, lt, self.at(x), :]

    def zp(self, v):
        return pltpu.roll(v, self.nz - 1, 0)

    def zm(self, v):
        return pltpu.roll(v, 1, 0)

    def edge(self, row, shift):
        wide = jnp.broadcast_to(row, (8, LANES))
        return jnp.concatenate(
            [pltpu.roll(wide, shift + 8 * z, 1, stride=8, stride_axis=0) for z in range(0, self.nz, 8)],
            axis=0,
        )

    def ym(self, a, h=None):
        r0, r1 = pltpu.roll(a[0], 1, 1), pltpu.roll(a[1], 1, 1)
        return r0 if h is None else jnp.where(self.first, h, r0), jnp.where(self.first, r0, r1)

    def yp(self, a, h=None):
        r0, r1 = pltpu.roll(a[0], LANES - 1, 1), pltpu.roll(a[1], LANES - 1, 1)
        return jnp.where(self.last, r1, r0), r1 if h is None else jnp.where(self.last, h, r1)

    def plane(self, x, p, w_ref, row=None):
        h = None if row is None else self.edge(row, 5)
        a, b = self.ym(p, h), self.yp(p, h)
        for lt in range(2):
            q = p[lt] + p[lt] + (a[lt] + b[lt])
            w_ref[0, lt, self.at(x), :] = p[lt]
            w_ref[1, lt, self.at(x), :] = q
            w_ref[2, lt, self.at(x), :] = q + (self.zp(p[lt]) + self.zm(p[lt]))
            w_ref[3, lt, self.at(x), :] = b[lt] - a[lt]

    def posts(self, x, lt, w, v):
        bb = w(1, lt, x) + (w(0, lt, x + 1) + w(0, lt, x - 1))
        dd = w(3, lt, x)
        fx = w(2, lt, x + 1) - w(2, lt, x - 1)
        fy = dd + dd + (self.zp(dd) + self.zm(dd)) + (w(3, lt, x + 1) + w(3, lt, x - 1))
        fz = self.zp(bb) - self.zm(bb)
        m = pushed(w(0, lt, x), (fx, fy, fz), [v(k, lt, x) for k in (1, 2, 3)])
        return post_of(v(0, lt, x), m)

    def half(self, x, other, lt, w, v):
        bb = w(1, lt, x) + w(0, lt, other)
        dd = w(3, lt, x)
        fx = w(2, lt, other) if other > x else -w(2, lt, other)
        fy = dd + dd + (self.zp(dd) + self.zm(dd)) + w(3, lt, other)
        fz = self.zp(bb) - self.zm(bb)
        return pushed(w(0, lt, x), (fx, fy, fz), [v(k, lt, x) for k in (1, 2, 3)])

    def rest(self, x, other, lt, w, v):
        p = w(0, lt, other)
        fx = w(2, lt, other) if other > x else -w(2, lt, other)
        fz = self.zp(p) - self.zm(p)
        m = pushed(w(0, lt, x), (fx, w(3, lt, other), fz), [v(k, lt, x) for k in (1, 2, 3)])
        return post_of(v(0, lt, x), m)

    def first_step(self, x, g_ref, posts):
        zp, zm = self.zp, self.zm
        part, left, right = [], [], []
        for lt in range(2):
            f = posts(lt)
            a15, a17, a18, a16 = zm(f[15]), zp(f[17]), zm(f[18]), zp(f[16])
            left.append((f[3] + (a15 + a17), a15 - a17, f[7], f[10]))
            right.append((f[4] + (a18 + a16), a18 - a16, f[9], f[8]))
            a, b = zm(f[5]), zp(f[6])
            s = [f[0] + (a + b), a - b]
            a, b = zm(f[11]), zp(f[13])
            s += [f[1] + (a + b), a - b]
            a, b = zm(f[14]), zp(f[12])
            s += [f[2] + (a + b), a - b]
            part.append(s)
        m = [self.ym((left[0][n], left[1][n])) for n in range(4)]
        q = [self.yp((right[0][n], right[1][n])) for n in range(4)]
        for lt in range(2):
            s = part[lt]

            def put(n, value):
                g_ref[n, lt, self.at(x), :] = value

            put(0, s[0] + (m[0][lt] + q[0][lt]))
            put(1, m[0][lt] - q[0][lt])
            put(2, s[1] + (m[1][lt] + q[1][lt]))
            put(3, s[2] + (m[2][lt] + q[2][lt]))
            put(4, m[2][lt] - q[2][lt])
            put(5, s[3])
            put(6, s[4] + (m[3][lt] + q[3][lt]))
            put(7, m[3][lt] - q[3][lt])
            put(8, s[5])

    def gather(self, x, g):
        out = []
        for lt in range(2):
            ru, rd = g(3, lt, x - 1), g(6, lt, x + 1)
            v = [g(0, lt, x) + (ru + rd), ru - rd]
            for k in (1, 2):
                v.append(g(k, lt, x) + (g(k + 3, lt, x - 1) + g(k + 6, lt, x + 1)))
            out.append(v)
        return out

    def patch(self, x, v, row, e_ref):
        for k in range(len(v[0])):
            h = self.edge(row(k), 4)
            v[0][k] = jnp.where(self.two[0], h, v[0][k])
            v[1][k] = jnp.where(self.two[1], h, v[1][k])
            for lt in range(2):
                e_ref[k, lt, self.at(x), :] = v[lt][k]
        return [density(v[0][0]), density(v[1][0])]

    def second_step(self, x, w, e, row, buf, shift):
        zp, zm = self.zp, self.zm
        left, right = [], []
        n, u, d = x + shift, x + shift + 1, x + shift - 1

        def put(i, row, lt, v):
            buf[row, i, :, lt * LANES : (lt + 1) * LANES] = v

        for lt in range(2):
            f = self.posts(x, lt, w, e)
            put(0, n, lt, f[0])
            put(5, n, lt, zm(f[5]))
            put(6, n, lt, zp(f[6]))
            put(1, u, lt, f[1])
            put(11, u, lt, zm(f[11]))
            put(13, u, lt, zp(f[13]))
            put(2, d, lt, f[2])
            put(12, d, lt, zp(f[12]))
            put(14, d, lt, zm(f[14]))
            left.append((f[3], zm(f[15]), zp(f[17]), f[7], f[10]))
            right.append((f[4], zp(f[16]), zm(f[18]), f[8], f[9]))
        h = [self.edge(row(5 + j), 5) for j in range(5)]
        for j, (i, to) in enumerate(((3, n), (15, n), (17, n), (7, u), (10, d))):
            v = self.ym((left[0][j], left[1][j]), h[j])
            put(i, to, 0, v[0])
            put(i, to, 1, v[1])
        for j, (i, to) in enumerate(((4, n), (16, n), (18, n), (8, d), (9, u))):
            v = self.yp((right[0][j], right[1][j]), h[j])
            put(i, to, 0, v[0])
            put(i, to, 1, v[1])


def early_kernel(nz, rows, rho_ref, mom_ref, w_ref, g_ref, e_ref, x_ref):
    r = Rows(nz)
    w, g = r.of(w_ref), r.of(g_ref)

    def v(k, lt, x):
        return rho_ref[lt, r.at(x), :] if k == 0 else mom_ref[k - 1, lt, r.at(x), :]

    def start(x):
        r.plane(x, [density(rho_ref[lt, r.at(x), :]) for lt in range(2)], w_ref)

    def first(x):
        r.first_step(x, g_ref, lambda lt: r.posts(x, lt, w, v))

    def middle(x):
        v = r.gather(x, g)
        for lt in range(2):
            for k in range(4):
                e_ref[k, lt, r.at(x), :] = v[lt][k]

    loop(0, rows, start, 16)
    for side, x, other in ((0, 0, 1), (1, rows - 1, rows - 2)):
        for lt in range(2):
            x_ref[side, r.at(8 + lt), :] = v(0, lt, x)
            for k, j in enumerate(r.half(x, other, lt, w, v)):
                x_ref[side, r.at(10 + 2 * k + lt), :] = j
    loop(1, rows - 1, first, 14)
    loop(2, rows - 2, middle, 12)
    for side, base, x, other in ((0, 6, 1, 2), (1, 3, rows - 2, rows - 3)):
        for lt in range(2):
            x_ref[side, r.at(lt), :] = g(0, lt, x) + g(base, lt, other)
            for k in range(3):
                x_ref[side, r.at(2 + 2 * k + lt), :] = g(base + k, lt, x)


def inner_kernel(nz, rows, e_in, o_ref, l_ref, r_ref, buf, e_ref, w_ref, s_ref):
    r = Rows(nz)
    strips_of_step(
        strips_of(
            [o_ref[k] for k in range(4)], [l_ref[k] for k in range(2)], [r_ref[k] for k in range(2)]
        ),
        s_ref,
    )

    def row(x):
        return lambda n: s_ref[n, pl.ds(x, 1), :]

    def middle(x):
        v = [[e_in[k, lt, r.at(x), :] for k in range(4)] for lt in range(2)]
        p = r.patch(x, v, row(x), e_ref)
        r.plane(x, p, w_ref, row(x)(4))

    def second(x):
        r.second_step(x, r.of(w_ref), r.of(e_ref), row(x), buf, -2)

    loop(2, rows - 2, middle, 12)
    loop(3, rows - 3, second, 10)


def outer_kernel(nz, rows, x_ref, o_ref, l_ref, r_ref, hl_ref, hr_ref, w0_in, g_in, e_in, w1_in, buf_in,
                 out_ref, w0_ref, g_ref, e_ref, w1_ref, s_ref, buf, sems):
    r = Rows(nz)

    def send(source, x):
        return pltpu.make_async_copy(source, out_ref.at[:, :, x, :], sems.at[x])

    inside = [send(buf_in.at[x - 2], x) for x in range(HALO, rows - HALO)]
    for copy in inside[:2]:
        copy.start()
    low = iota((8, LANES), 0) < HALO

    def with_halo(local, t, upper):
        at = pl.ds(16 * nz + 8 * t, 8)
        hl, hr = hl_ref[at, :], hr_ref[at, :]
        if upper:
            tile = jnp.where(low, pltpu.roll(hr, HALO, 0), hl)
        else:
            tile = jnp.where(low, hr, pltpu.roll(hl, HALO, 0))
        return jnp.concatenate([local, tile], axis=0)

    strips_of_step(
        strips_of(
            [with_halo(o_ref[k], 2 + k % 2, k >= 2) for k in range(4)],
            [with_halo(l_ref[k], k, False) for k in range(2)],
            [with_halo(r_ref[k], k, True) for k in range(2)],
        ),
        s_ref,
    )
    ring = rows + 2 * HALO

    def x_of(l):
        return l - HALO if l < 10 else l - 16 + rows

    def row(l):
        return lambda n: s_ref[n, pl.ds(x_of(l) % ring, 1), :]

    def either(ref, ref_in, inside):
        def get(n, lt, l):
            if inside <= x_of(l) < rows - inside:
                return ref_in[n, lt, r.at(x_of(l)), :]
            return ref[n, lt, r.at(l), :]

        return get

    def edge(l):
        ref = {3: hl_ref, 4: x_ref.at[0], 15: x_ref.at[1], 16: hr_ref}[l]
        return lambda k, lt, x: ref[r.at(8 + 2 * k + lt), :]

    w0 = either(w0_ref, w0_in, 0)
    for l in (3, 16):
        r.plane(l, [density(edge(l)(0, lt, l)) for lt in range(2)], w0_ref)
    for l, other in ((4, 3), (15, 16), (3, 4), (16, 15)):
        r.first_step(l, g_ref, lambda lt: r.rest(l, other, lt, w0, edge(l)))

    for copy in inside[2:]:
        copy.start()
    own = either(g_ref, g_in, 1)

    def g(n, lt, l):
        if l == 2 or l == 17:
            ref = hl_ref if l == 2 else hr_ref
            return ref[r.at(2 + 2 * (n % 3) + lt), :]
        return own(n, lt, l)

    for l in (5, 14, 4, 15, 3, 16):
        p = r.patch(l, r.gather(l, g), row(l), e_ref)
        r.plane(l, p, w1_ref, row(l)(4))

    for l, ref, n, near in ((2, hl_ref, 6, 3), (17, hr_ref, 3, 16)):
        v = [[ref[r.at(lt), :] + g_ref[n, lt, r.at(near), :]] for lt in range(2)]
        r.plane(l, r.patch(l, v, row(l), e_ref), w1_ref, row(l)(4))
    for l, x, indices in (
        (6, 2, LEFT),
        (7, 3, STILL + LEFT),
        (12, rows - 4, STILL + RIGHT),
        (13, rows - 3, RIGHT),
    ):
        for i in indices:
            buf[l, i] = buf_in[x - 2, i]

    w1, e = either(w1_ref, w1_in, 2), either(e_ref, e_in, 2)
    edges = []
    for side in range(2):
        for n in (3, 2, 1, 0):
            l, x = ((n + 3, n), (16 - n, rows - 1 - n))[side]
            r.second_step(l, w1, e, row(l), buf, 0)
            edges.append(send(buf.at[l + 1 if x == n else l - 1], x))
            edges[-1].start()
    for copy in inside + edges:
        copy.wait()


def body(populations):
    _, nz, rows, columns = populations.shape
    f32 = jnp.float32
    even_x = (lax.axis_index("gx") & 1) == 0
    even_y = (lax.axis_index("gy") & 1) == 0
    vmem = pl.BlockSpec(memory_space=pltpu.VMEM)
    hbm = pl.BlockSpec(memory_space=pltpu.HBM)
    chunks = 4
    params = pltpu.CompilerParams(vmem_limit_bytes=40 * 1024 * 1024)

    def shape(*dims):
        return jax.ShapeDtypeStruct(dims, f32)

    def field(n, count):
        return (n, 2, count * nz, LANES)

    def moments(*refs):
        moments_kernel(nz, chunks, *refs)

    rho, mom, o, to_left, to_right = pl.pallas_call(
        moments,
        out_shape=(
            shape(2, rows * nz, LANES), shape(*field(3, rows)), shape(4, rows, LANES),
            shape(2, rows, LANES), shape(2, rows, LANES),
        ),
        in_specs=[hbm],
        out_specs=(vmem, vmem, vmem, vmem, vmem),
        scratch_shapes=[
            pltpu.VMEM(populations.shape, populations.dtype),
            pltpu.SemaphoreType.DMA((chunks,)),
        ],
        compiler_params=pltpu.CompilerParams(vmem_limit_bytes=50 * 1024 * 1024),
        name="moments",
    )(pltpu.with_memory_space_constraint(populations, pltpu.HBM))

    def both(array_odd, array_even, axis):
        odd = pair_swap(array_odd, axis, 1)
        even = pair_swap(array_even, axis, 0)
        odd = lax.optimization_barrier(-odd)
        return -odd, even

    ob, oa = both(
        jnp.where(even_y, to_left, to_right), jnp.where(even_y, to_right, to_left), "gy"
    )

    left, right = jnp.where(even_y, ob, oa), jnp.where(even_y, oa, ob)

    def early(*refs):
        early_kernel(nz, rows, *refs)

    w0, g, e0, edges = pl.pallas_call(
        early,
        out_shape=(
            shape(*field(4, rows)), shape(*field(9, rows)), shape(*field(4, rows)),
            shape(2, 16 * nz, LANES),
        ),
        in_specs=[vmem, vmem],
        out_specs=(vmem, vmem, vmem, vmem),
        compiler_params=params,
        cost_estimate=pl.CostEstimate(flops=10_000_000, bytes_accessed=2_500_000, transcendentals=0),
        name="early",
    )(rho, mom)

    left, right, edges, e0 = lax.optimization_barrier((left, right, edges, e0))

    def edge(low):
        c = slice(0, HALO) if low else slice(rows - HALO, rows)
        return jnp.concatenate([
            edges[0 if low else 1],
            jnp.concatenate([left[:, c], right[:, c]], axis=1).reshape(-1, LANES),
            jnp.concatenate([o[:2, c], o[2:, c]], axis=1).reshape(-1, LANES),
        ])

    low, high = edge(True), edge(False)
    hb, ha = both(jnp.where(even_x, low, high), jnp.where(even_x, high, low), "gx")

    def inner(*refs):
        inner_kernel(nz, rows, *refs)

    buf, e, w1 = pl.pallas_call(
        inner,
        out_shape=(
            shape(rows - HALO, 19, nz, columns), shape(*field(4, rows)), shape(*field(4, rows)),
        ),
        in_specs=[vmem] * 4,
        out_specs=(vmem, vmem, vmem),
        scratch_shapes=[pltpu.VMEM((10, rows, LANES), f32)],
        compiler_params=params,
        cost_estimate=pl.CostEstimate(flops=10_000_000, bytes_accessed=2_500_000, transcendentals=0),
        name="inner",
    )(e0, o, left, right)
    hl, hr = jnp.where(even_x, hb, ha), jnp.where(even_x, ha, hb)

    def outer(*refs):
        outer_kernel(nz, rows, *refs)

    ring = rows + 2 * HALO
    return pl.pallas_call(
        outer,
        out_shape=shape(*populations.shape),
        in_specs=[vmem] * 11,
        out_specs=hbm,
        scratch_shapes=[
            pltpu.VMEM(field(4, 20), f32),
            pltpu.VMEM(field(9, 20), f32),
            pltpu.VMEM(field(4, 20), f32),
            pltpu.VMEM(field(4, 20), f32),
            pltpu.VMEM((10, ring, LANES), f32),
            pltpu.VMEM((20, 19, nz, columns), f32),
            pltpu.SemaphoreType.DMA((rows,)),
        ],
        compiler_params=params,
        name="outer",
    )(edges, o, left, right, hl, hr, w0, g, e, w1, buf)


def solution(mesh):
    return jax.shard_map(
        body,
        mesh=mesh,
        in_specs=(P(None, None, "gx", "gy"),),
        out_specs=P(None, None, "gx", "gy"),
        check_vma=False,
    )
```
